256 devices in a mesh: dp: 4 (over y), tensor: 16 (over z, x_hi), query: 4 (over x_lo, core).
Axes of the slice: x: 4 (x_hi: 2, x_lo: 2; x = x_hi * 2 + x_lo), y: 4, z: 8, core: 2. Of those that a mesh axis runs over, the one named last changes fastest.
Arguments:
- activations: bfloat16 [64, 512, 28672], P(('dp', 'query'), None, 'tensor'), may hold values from -6 to 6
- out_grads: bfloat16 [64, 512, 8192], P(('dp', 'query'), None, 'tensor'), may hold values from -6 to 6
- token_mask: int32 [64, 512], P(('dp', 'query')), may hold values 0 or 1
- in_proj: bfloat16 [28672, 64], P('tensor'), may hold values from -0.03125 to 0.03125
- out_proj: bfloat16 [8192, 64], P('tensor'), may hold values from -0.0625 to 0.0625
- output_inverse_factor: float32 [64, 64], replicated, may hold values from -0.6 to 3.6, as said below
- input_inverse_factor: float32 [64, 64], replicated, may hold values from -0.6 to 3.6, as said below
- query_grads: float32 [32, 16, 4096], P('query', 'dp', 'tensor'), may hold values from -2 to 2
Outputs:
- scores: float32 [64, 32, 16], P(('dp', 'query'), None, 'tensor')
The draws below stay inside these ranges and needn't reach their ends.
Inputs may be any that keep to these rules, and one draw needn't show every extreme that they name: `output_inverse_factor`: each factor is its diagonal, between 1 and 3, plus entries of at most 0.6 in magnitude. `input_inverse_factor`: each factor is its diagonal, between 1 and 3, plus entries of at most 0.6 in magnitude.
All inputs are finite; a program needn't handle non-finite values. No bound on the sum of `token_mask` on one device may be relied on, other than what follows from the above.
Results may differ from the reference program's by a relative error of at most 0.0003.
Values sent between devices are 32-bit elements; how exact they have to be, the bound alone decides.
A program may use at most 64 MiB of HBM per device.

```python
import jax
import jax.numpy as jnp
from jax import lax

D = 8192
FF = 28672
R = 64
LEN = 512
RR = 4096
DOCS = 64
QUERY_ROWS = 32
QUERY_COLS = 16


def factor_draw(key):
    key_diag, key_offset = jax.random.split(key)
    diag_vals = jax.random.uniform(key_diag, (R,), jnp.float32, 1.0, 3.0)
    off_vals = jnp.clip(0.15 * jax.random.normal(key_offset, (R, R), jnp.float32), -0.6, 0.6)
    return jnp.eye(R, dtype=jnp.float32) * diag_vals[None, :] + off_vals


def draw_output_inverse_factor(key, part):
    key = jax.random.fold_in(key, 11)
    return factor_draw(key)


def draw_input_inverse_factor(key, part):
    key = jax.random.fold_in(key, 23)
    return factor_draw(key)


def with_ends(drawn, stream_key, low, high):
    longest = drawn.shape.index(max(drawn.shape))
    spots = []
    for shift in (0, 1):
        where = [jax.random.randint(jax.random.fold_in(stream_key, axis), (), 0, length) for axis, length in enumerate(drawn.shape)]
        where[longest] = (where[longest] + shift) % drawn.shape[longest]
        spots.append(tuple(where))
    return drawn.at[spots[0]].set(low).at[spots[1]].set(high)


def steps_of(own_key, shape, pieces, least, top_value):
    level = 1.0
    for dim, parts in pieces:
        heights = jax.random.uniform(jax.random.fold_in(jax.random.fold_in(own_key, 6), dim), (parts,), jnp.float32, least / len(pieces), top_value / len(pieces))
        level = level * jnp.repeat(jnp.exp(heights), shape[dim] // parts).reshape((-1,) + (1,) * (len(shape) - 1 - dim))
    return level


def normal_values(stream_key, extent, width, most, cuts=(), kind=jnp.bfloat16):
    array = width * jax.random.normal(stream_key, extent, jnp.float32)
    if cuts:
        array = array * steps_of(stream_key, extent, cuts, -0.22, 0.18)
    return jnp.clip(array, -most, most).astype(kind)


def setup_inputs(seed: int = 0) -> dict:
    keys = jax.random.split(jax.random.key(seed), 9)
    activations = normal_values(keys[0], (DOCS, LEN, FF), 1.0, 6.0, ((0, 16), (2, 16)))
    out_grads = normal_values(keys[1], (DOCS, LEN, D), 1.0, 6.0, ((0, 16), (2, 16)))
    token_mask = with_ends((jax.random.randint(keys[2], (DOCS, LEN), 0, 4) < 3).astype(jnp.int32), jax.random.fold_in(keys[2], 1), 0, 1)
    in_proj = normal_values(keys[3], (FF, R), FF ** -0.5, 0.03125, ((0, 16),))
    out_proj = normal_values(keys[4], (D, R), D ** -0.5, 0.0625, ((0, 16),))
    output_inverse_factor = draw_output_inverse_factor(jax.random.fold_in(keys[8], 71), 0)
    input_inverse_factor = draw_input_inverse_factor(jax.random.fold_in(keys[8], 71), 0)
    query_grads = normal_values(keys[7], (QUERY_ROWS, QUERY_COLS, RR), 0.25, 2.0, ((0, 4), (1, 4), (2, 16)), jnp.float32)
    return dict(activations=activations, out_grads=out_grads, token_mask=token_mask, in_proj=in_proj, out_proj=out_proj, output_inverse_factor=output_inverse_factor, input_inverse_factor=input_inverse_factor, query_grads=query_grads)


def reference(activations, out_grads, token_mask, in_proj, out_proj, output_inverse_factor, input_inverse_factor, query_grads):
    weights = token_mask.astype(jnp.float32) / LEN

    def per_doc(item):
        act, grad, down_weight = item
        proj_in = jnp.dot(act, in_proj, preferred_element_type=jnp.float32)
        proj_out = jnp.dot(grad, out_proj, preferred_element_type=jnp.float32)
        return jnp.einsum('ti,tj->ij', proj_out * down_weight[:, None], proj_in, precision=lax.Precision.HIGHEST)

    document_gradients = lax.map(per_doc, (activations, out_grads, weights))
    preconditioned_grads = jnp.einsum('ms,qsc->qmc', output_inverse_factor, document_gradients, precision=lax.Precision.HIGHEST)
    preconditioned_grads = jnp.einsum('xoh,hu->xou', preconditioned_grads, input_inverse_factor, precision=lax.Precision.HIGHEST)
    flat = preconditioned_grads.reshape(DOCS, R * R)
    return jnp.einsum('df,rcf->drc', flat, query_grads, precision=lax.Precision.HIGHEST)
```

```python
import functools

import jax
import jax.numpy as jnp
from jax import lax
from jax.experimental import pallas as pl
from jax.experimental.pallas import tpu as pltpu
from jax.sharding import PartitionSpec as P

MESH = pl.DeviceIdType.MESH
F32 = jnp.float32
HIGH = lax.Precision.HIGHEST
ORDER = (4, 3, -3, 2, -2, 1, -1, 0)
LAG = 3


def nt(a, b, precision=None):
    return lax.dot_general(
        a, b, (((1,), (1,)), ((), ())), precision=precision, preferred_element_type=F32
    )


def tn(a, b, precision=None):
    return lax.dot_general(
        a, b, (((0,), (0,)), ((), ())), precision=precision, preferred_element_type=F32
    )


def kernel(
    act, grads, mask, w_in, w_out, f_out, f_in, query, out,
    act_v, grads_v, mask_v, w_in_v, w_out_v, f_out_v, f_in_v, query_v,
    parts, x_got, z_got, q_all, c_send, c_got, s_send, s_got,
    load_sem, x_send, x_recv, z_send, z_recv, q_send, q_recv,
    c_send_sem, c_recv_sem, s_send_sem, s_recv_sem,
):
    dp = lax.axis_index("dp")
    me = lax.axis_index("tensor")
    qi = lax.axis_index("query")
    z, a = me // 2, lax.rem(me, 2)
    x_lo, core = qi // 2, lax.rem(qi, 2)

    def tensor_peer(k):
        return {"tensor": lax.rem(me + k, 16)}

    def dp_peer(k):
        return {"dp": lax.rem(dp + k, 4)}

    lo_peer = {"query": (1 - x_lo) * 2 + core}
    core_peer = {"query": x_lo * 2 + 1 - core}
    x_peer = {"tensor": z * 2 + 1 - a}

    barrier = pltpu.get_barrier_semaphore()
    peers = [tensor_peer(k) for k in range(1, 16)] + [dp_peer(k) for k in (1, 2, 3)]
    peers += [lo_peer, core_peer]
    for peer in peers:
        pl.semaphore_signal(barrier, inc=1, device_id=peer, device_id_type=MESH)

    def load(src, dst, n):
        copy = pltpu.make_async_copy(src, dst, load_sem.at[n])
        copy.start()
        return copy

    load_w_in = load(w_in, w_in_v, 0)
    load_w_out = load(w_out, w_out_v, 1)
    load_rows = []
    for n, k in enumerate(ORDER):
        owner = lax.rem(z + k + 8, 8)
        rows = pl.ds(pl.multiple_of(owner * 256, 256), 256)
        load_rows.append(
            (
                load(act.at[rows], act_v.at[n], 7 + 2 * n),
                load(grads.at[rows], grads_v.at[n], 8 + 2 * n),
            )
        )
        if n == 0:
            load_query = load(query, query_v, 2)
    load_mask = load(mask, mask_v, 3)
    load_f_out = load(f_out, f_out_v, 4)
    load_f_in = load(f_in, f_in_v, 5)

    def remote(src, dst, send, recv, peer):
        return pltpu.make_async_remote_copy(
            src_ref=src, dst_ref=dst, send_sem=send, recv_sem=recv, device_id=peer, device_id_type=MESH
        )

    load_query.wait()
    my_columns = pl.ds(pl.multiple_of(dp * 4, 4), 4)
    my_rows = pl.ds(pl.multiple_of(qi * 8, 8), 8)
    for j in range(4):
        q_all[dp * 4 + j, my_rows, :] = query_v[:, j, :]

    load_w_in.wait()
    load_w_out.wait()

    x_copies, z_copies = [], []

    def project(n):
        for copy in load_rows[n]:
            copy.wait()
        p_in = nt(w_in_v[...], act_v[n])
        p_out = nt(w_out_v[...], grads_v[n])
        for half in range(2):
            lanes = slice(128 * half, 128 * half + 128)
            parts[2 * n + half, 0:64, :] = p_in[:, lanes]
            parts[2 * n + half, 64:128, :] = p_out[:, lanes]

    def send_x(n):
        copy = remote(parts.at[2 * n + 1 - a], x_got.at[n], x_send.at[n], x_recv.at[n], x_peer)
        copy.start()
        x_copies.append(copy)

    def second(n):
        x_copies[n].wait_recv()
        both = parts[2 * n + a] + x_got[n]
        if ORDER[n] == 0:
            return both
        parts[2 * n + a] = both
        peer = {"tensor": lax.rem(z + ORDER[n] + 8, 8) * 2 + a}
        copy = remote(parts.at[2 * n + a], z_got.at[n], z_send.at[n], z_recv.at[n], peer)
        copy.start()
        z_copies.append(copy)
        return None

    project(0)
    pl.semaphore_wait(barrier, len(peers))
    send_x(0)

    block = q_all.at[my_columns, my_rows]
    q_copies = [remote(block, block, q_send.at[k - 1], q_recv.at[k - 1], dp_peer(k)) for k in (1, 2, 3)]
    for copy in q_copies:
        copy.start()

    total = None
    for n in range(1, 8):
        project(n)
        send_x(n)
        if n >= LAG:
            total = second(n - LAG)

    for copy in q_copies:
        copy.wait_recv()
    block = q_all.at[:, my_rows]
    lo_copy = remote(block, block, q_send.at[3], q_recv.at[3], lo_peer)
    lo_copy.start()

    for n in range(8 - LAG, 8):
        total = second(n)

    lo_copy.wait_recv()
    core_copies = []
    for half in range(2):
        rows = pl.ds(pl.multiple_of((half * 2 + core) * 8, 8), 8)
        block = q_all.at[:, rows]
        copy = remote(block, block, q_send.at[4 + half], q_recv.at[4 + half], core_peer)
        copy.start()
        core_copies.append(copy)

    load_mask.wait()
    load_f_out.wait()
    load_f_in.wait()
    weights = jnp.zeros((1, 128), F32)
    for n in range(16):
        piece = mask_v[n // 4 : n // 4 + 1, 128 * (n % 4) : 128 * (n % 4) + 128].astype(F32)
        weights = jnp.where(me == n, piece / 512.0, weights)

    for n in range(7):
        z_copies[n].wait_recv()
        total = total + z_got[n]

    side_out = jnp.dot(f_out_v[...], total[64:128] * weights, precision=HIGH, preferred_element_type=F32)
    side_in = tn(f_in_v[...], total[0:64], HIGH)
    conditioned = nt(side_out, side_in, HIGH)

    c_send[...] = conditioned.reshape(16, 4, 64)
    far_first = sorted(range(1, 16), key=lambda k: -min(k // 2, 8 - k // 2))
    c_copies = []
    for k in far_first:
        peer = lax.rem(me + k, 16)
        copy = remote(c_send.at[peer], c_got.at[me], c_send_sem.at[k - 1], c_recv_sem.at[k - 1], tensor_peer(k))
        copy.start()
        c_copies.append(copy)
    c_got[me] = c_send[me]
    for copy in core_copies:
        copy.wait_recv()
    q = q_all[...].reshape(512, 256)
    for copy in c_copies[::-1]:
        copy.wait_recv()
    mine = c_got[...].reshape(4, 4, 4, 64)
    mine = mine[:, 0] + mine[:, 1] + mine[:, 2] + mine[:, 3]
    mine = jnp.concatenate([mine[:, i] for i in range(4)], axis=-1)

    scores = nt(mine, q, HIGH)
    for c in range(16):
        s_send[c] = scores[:, 32 * c : 32 * c + 32]
    s_copies = []
    for k in far_first:
        peer = lax.rem(me + k, 16)
        copy = remote(s_send.at[peer], s_got.at[me], s_send_sem.at[k - 1], s_recv_sem.at[k - 1], tensor_peer(k))
        copy.start()
        s_copies.append(copy)
    s_got[me] = s_send[me]
    for copy in s_copies[::-1]:
        copy.wait_recv()
    out[...] = jnp.sum(s_got[...], axis=0)

    for copy in x_copies + z_copies + q_copies + [lo_copy] + core_copies + c_copies + s_copies:
        copy.wait_send()


def local(act, grads, mask, w_in, w_out, f_out, f_in, query):
    docs, length, hidden = act.shape
    model = grads.shape[2]
    vmem, sem = pltpu.VMEM, pltpu.SemaphoreType.DMA
    scores = pl.pallas_call(
        kernel,
        name="influence",
        out_shape=jax.ShapeDtypeStruct((4, 32), F32),
        in_specs=[pl.BlockSpec(memory_space=pl.ANY)] * 8,
        out_specs=pl.BlockSpec(memory_space=pltpu.VMEM),
        scratch_shapes=[
            vmem((8, 256, hidden), jnp.bfloat16),
            vmem((8, 256, model), jnp.bfloat16),
            vmem((4, 512), jnp.int32),
            vmem((64, hidden), jnp.bfloat16),
            vmem((64, model), jnp.bfloat16),
            vmem((64, 64), F32),
            vmem((64, 64), F32),
            vmem((8, 4, 256), F32),
            vmem((16, 128, 128), F32),
            vmem((8, 128, 128), F32),
            vmem((7, 128, 128), F32),
            vmem((16, 32, 256), F32),
            vmem((16, 4, 64), F32),
            vmem((16, 4, 64), F32),
            vmem((16, 4, 32), F32),
            vmem((16, 4, 32), F32),
            sem((23,)),
            sem((8,)), sem((8,)),
            sem((7,)), sem((7,)),
            sem((6,)), sem((6,)),
            sem((15,)), sem((15,)),
            sem((15,)), sem((15,)),
        ],
        compiler_params=pltpu.CompilerParams(
            collective_id=0, has_side_effects=True, vmem_limit_bytes=56 * 2**20
        ),
    )(
        act.reshape(docs * length, hidden),
        grads.reshape(docs * length, model),
        mask, w_in.T, w_out.T, f_out, f_in, query,
    )
    return scores.reshape(4, 32, 1)


def solution(mesh):
    placed = (
        P(("dp", "query"), None, "tensor"),
        P(("dp", "query"), None, "tensor"),
        P(("dp", "query"), None),
        P("tensor", None),
        P("tensor", None),
        P(),
        P(),
        P("query", "dp", "tensor"),
    )
    return jax.shard_map(
        local,
        mesh=mesh,
        in_specs=placed,
        out_specs=P(("dp", "query"), None, "tensor"),
        check_vma=False,
    )
```

```python
import functools

import jax
import jax.numpy as jnp
from jax import lax
from jax.experimental import pallas as pl
from jax.experimental.pallas import tpu as pltpu
from jax.sharding import PartitionSpec as P

MESH = pl.DeviceIdType.MESH
F32 = jnp.float32
HIGH = lax.Precision.HIGHEST
ORDER = (4, 3, 1, -3, -1, 2, -2, 0)


def nt(a, b, precision=None):
    return lax.dot_general(
        a, b, (((1,), (1,)), ((), ())), precision=precision, preferred_element_type=F32
    )


def tn(a, b, precision=None):
    return lax.dot_general(
        a, b, (((0,), (0,)), ((), ())), precision=precision, preferred_element_type=F32
    )


def kernel(
    act, grads, mask, w_in, w_out, f_out, f_in, query, out,
    act_v, grads_v, mask_v, w_in_v, w_out_v, f_out_v, f_in_v, query_v,
    parts, x_got, near_got, three_got, four_got, two_got, q_all, c_send, c_got, s_send, s_got,
    load_sem, x_send, x_recv, z_send, z_recv, q_send, q_recv,
    c_send_sem, c_recv_sem, s_send_sem, s_recv_sem,
):
    dp = lax.axis_index("dp")
    me = lax.axis_index("tensor")
    qi = lax.axis_index("query")
    z, a = me // 2, lax.rem(me, 2)
    x_lo, core = qi // 2, lax.rem(qi, 2)

    def tensor_peer(k):
        return {"tensor": lax.rem(me + k, 16)}

    def dp_peer(k):
        return {"dp": lax.rem(dp + k, 4)}

    def z_peer(k):
        return {"tensor": lax.rem(z + k + 8, 8) * 2 + a}

    lo_peer = {"query": (1 - x_lo) * 2 + core}
    core_peer = {"query": x_lo * 2 + 1 - core}
    x_peer = {"tensor": z * 2 + 1 - a}

    barrier = pltpu.get_barrier_semaphore()
    peers = [x_peer] + [z_peer(k) for k in (1, -1, 2, -2)] + [lo_peer, core_peer]
    peers += [dp_peer(k) for k in (1, 2, 3)]
    for peer in peers:
        pl.semaphore_signal(barrier, inc=1, device_id=peer, device_id_type=MESH)

    def load(src, dst, n):
        copy = pltpu.make_async_copy(src, dst, load_sem.at[n])
        copy.start()
        return copy

    load_w_in = load(w_in, w_in_v, 0)
    load_w_out = load(w_out, w_out_v, 1)
    load_rows = []
    for n, k in enumerate(ORDER):
        owner = lax.rem(z + k + 8, 8)
        rows = pl.ds(pl.multiple_of(owner * 256, 256), 256)
        load_rows.append(
            (
                load(act.at[rows], act_v.at[n], 7 + 2 * n),
                load(grads.at[rows], grads_v.at[n], 8 + 2 * n),
            )
        )
        if n == 0:
            load_query = load(query, query_v, 2)
    load_mask = load(mask, mask_v, 3)
    load_f_out = load(f_out, f_out_v, 4)
    load_f_in = load(f_in, f_in_v, 5)

    started = []

    def remote(src, dst, send, recv, peer):
        copy = pltpu.make_async_remote_copy(
            src_ref=src, dst_ref=dst, send_sem=send, recv_sem=recv, device_id=peer, device_id_type=MESH
        )
        copy.start()
        started.append(copy)
        return copy

    def project(k):
        n = ORDER.index(k)
        for copy in load_rows[n]:
            copy.wait()
        p_in = nt(w_in_v[...], act_v[n])
        p_out = nt(w_out_v[...], grads_v[n])
        for half in range(2):
            lanes = slice(128 * half, 128 * half + 128)
            parts[2 * n + half, 0:64, :] = p_in[:, lanes]
            parts[2 * n + half, 64:128, :] = p_out[:, lanes]

    def mine(k):
        return 2 * ORDER.index(k) + a

    def other(k):
        return 2 * ORDER.index(k) + 1 - a

    x_copies = {}

    def send_x(k):
        n = ORDER.index(k)
        x_copies[k] = remote(parts.at[other(k)], x_got.at[n], x_send.at[n], x_recv.at[n], x_peer)

    def add_x(k):
        x_copies[k].wait_recv()
        parts[mine(k)] = parts[mine(k)] + x_got[ORDER.index(k)]

    def send_z(n, src, dst, k):
        return remote(src, dst, z_send.at[n], z_recv.at[n], z_peer(k))

    load_w_in.wait()
    load_w_out.wait()
    project(4)
    load_query.wait()
    my_columns = pl.ds(pl.multiple_of(dp * 4, 4), 4)
    for j in range(4):
        q_all[dp * 4 + j, x_lo, core] = query_v[:, j, :]

    pl.semaphore_wait(barrier, len(peers))
    send_x(4)
    block = q_all.at[my_columns, x_lo, core]
    lo_copy = remote(block, block, q_send.at[0], q_recv.at[0], lo_peer)
    project(3)
    send_x(3)
    project(1)
    n = 2 * ORDER.index(1)
    near_up = send_z(0, parts.at[n : n + 2], near_got.at[0], 1)
    project(-3)
    send_x(-3)
    project(-1)
    n = 2 * ORDER.index(-1)
    near_down = send_z(1, parts.at[n : n + 2], near_got.at[1], -1)
    lo_copy.wait_recv()
    block = q_all.at[my_columns, :, core]
    q_copies = [remote(block, block, q_send.at[k], q_recv.at[k], dp_peer(k)) for k in (1, 2, 3)]
    add_x(4)
    four_up = send_z(2, parts.at[mine(4), 0:64], four_got.at[0], 2)
    four_down = send_z(3, parts.at[mine(4), 64:128], four_got.at[1], -2)
    project(2)
    send_x(2)
    project(-2)
    send_x(-2)
    add_x(3)
    three_up = send_z(4, parts.at[mine(3)], three_got.at[0], 1)
    project(0)
    add_x(-3)
    three_down = send_z(5, parts.at[mine(-3)], three_got.at[1], -1)
    near_up.wait_recv()
    near_down.wait_recv()
    parts[other(0)] = parts[other(0)] + near_got[0, 1 - a] + near_got[1, 1 - a]
    send_x(0)
    add_x(2)
    three_up.wait_recv()
    four_up.wait_recv()
    n = mine(2)
    parts[n, 0:64] = parts[n, 0:64] + three_got[0, 0:64] + four_got[0]
    parts[n, 64:128] = parts[n, 64:128] + three_got[0, 64:128]
    two_up = send_z(6, parts.at[n], two_got.at[0], 2)
    add_x(-2)
    three_down.wait_recv()
    four_down.wait_recv()
    n = mine(-2)
    parts[n, 0:64] = parts[n, 0:64] + three_got[1, 0:64]
    parts[n, 64:128] = parts[n, 64:128] + three_got[1, 64:128] + four_got[1]
    two_down = send_z(7, parts.at[n], two_got.at[1], -2)

    for copy in q_copies:
        copy.wait_recv()
    block = q_all.at[:, :, core]
    core_copy = remote(block, block, q_send.at[4], q_recv.at[4], core_peer)
    total = parts[mine(0)] + near_got[0, a] + near_got[1, a]

    load_mask.wait()
    load_f_out.wait()
    load_f_in.wait()
    weights = jnp.zeros((1, 128), F32)
    for n in range(16):
        piece = mask_v[n // 4 : n // 4 + 1, 128 * (n % 4) : 128 * (n % 4) + 128].astype(F32)
        weights = jnp.where(me == n, piece / 512.0, weights)

    x_copies[0].wait_recv()
    total = total + x_got[ORDER.index(0)]
    two_up.wait_recv()
    total = total + two_got[0]
    two_down.wait_recv()
    total = total + two_got[1]

    side_out = jnp.dot(f_out_v[...], total[64:128] * weights, precision=HIGH, preferred_element_type=F32)
    side_in = tn(f_in_v[...], total[0:64], HIGH)
    conditioned = nt(side_out, side_in, HIGH)

    c_send[...] = conditioned.reshape(16, 4, 64)
    far_first = sorted(range(1, 16), key=lambda k: -min(k // 2, 8 - k // 2))
    c_copies = []
    for k in far_first:
        peer = lax.rem(me + k, 16)
        copy = remote(c_send.at[peer], c_got.at[me], c_send_sem.at[k - 1], c_recv_sem.at[k - 1], tensor_peer(k))
        c_copies.append(copy)
    c_got[me] = c_send[me]
    core_copy.wait_recv()
    q = q_all[...].reshape(512, 256)
    for copy in c_copies[::-1]:
        copy.wait_recv()
    got = c_got[...].reshape(4, 4, 4, 64)
    got = got[:, 0] + got[:, 1] + got[:, 2] + got[:, 3]
    got = jnp.concatenate([got[:, i] for i in range(4)], axis=-1)

    scores = nt(got, q, HIGH)
    for c in range(16):
        s_send[c] = scores[:, 32 * c : 32 * c + 32]
    s_copies = []
    for k in far_first:
        peer = lax.rem(me + k, 16)
        copy = remote(s_send.at[peer], s_got.at[me], s_send_sem.at[k - 1], s_recv_sem.at[k - 1], tensor_peer(k))
        s_copies.append(copy)
    s_got[me] = s_send[me]
    for copy in s_copies[::-1]:
        copy.wait_recv()
    out[...] = jnp.sum(s_got[...], axis=0)

    for copy in started:
        copy.wait_send()


def local(act, grads, mask, w_in, w_out, f_out, f_in, query):
    docs, length, hidden = act.shape
    model = grads.shape[2]
    vmem, sem = pltpu.VMEM, pltpu.SemaphoreType.DMA
    scores = pl.pallas_call(
        kernel,
        name="influence",
        out_shape=jax.ShapeDtypeStruct((4, 32), F32),
        in_specs=[pl.BlockSpec(memory_space=pl.ANY)] * 8,
        out_specs=pl.BlockSpec(memory_space=pltpu.VMEM),
        scratch_shapes=[
            vmem((8, 256, hidden), jnp.bfloat16),
            vmem((8, 256, model), jnp.bfloat16),
            vmem((4, 512), jnp.int32),
            vmem((64, hidden), jnp.bfloat16),
            vmem((64, model), jnp.bfloat16),
            vmem((64, 64), F32),
            vmem((64, 64), F32),
            vmem((8, 4, 256), F32),
            vmem((16, 128, 128), F32),
            vmem((8, 128, 128), F32),
            vmem((2, 2, 128, 128), F32),
            vmem((2, 128, 128), F32),
            vmem((2, 64, 128), F32),
            vmem((2, 128, 128), F32),
            vmem((16, 2, 2, 8, 256), F32),
            vmem((16, 4, 64), F32),
            vmem((16, 4, 64), F32),
            vmem((16, 4, 32), F32),
            vmem((16, 4, 32), F32),
            sem((23,)),
            sem((8,)), sem((8,)),
            sem((8,)), sem((8,)),
            sem((5,)), sem((5,)),
            sem((15,)), sem((15,)),
            sem((15,)), sem((15,)),
        ],
        compiler_params=pltpu.CompilerParams(
            collective_id=0, has_side_effects=True, vmem_limit_bytes=56 * 2**20
        ),
    )(
        act.reshape(docs * length, hidden),
        grads.reshape(docs * length, model),
        mask, w_in.T, w_out.T, f_out, f_in, query,
    )
    return scores.reshape(4, 32, 1)


def solution(mesh):
    placed = (
        P(("dp", "query"), None, "tensor"),
        P(("dp", "query"), None, "tensor"),
        P(("dp", "query"), None),
        P("tensor", None),
        P("tensor", None),
        P(),
        P(),
        P("query", "dp", "tensor"),
    )
    return jax.shard_map(
        local,
        mesh=mesh,
        in_specs=placed,
        out_specs=P(("dp", "query"), None, "tensor"),
        check_vma=False,
    )
```

```python
import functools

import jax
import jax.numpy as jnp
from jax import lax
from jax.experimental import pallas as pl
from jax.experimental.pallas import tpu as pltpu
from jax.sharding import PartitionSpec as P

MESH = pl.DeviceIdType.MESH
F32 = jnp.float32
HIGH = lax.Precision.HIGHEST
ORDER = (4, 3, 1, -3, -1, 2, -2, 0)


def nt(a, b, precision=None):
    return lax.dot_general(
        a, b, (((1,), (1,)), ((), ())), precision=precision, preferred_element_type=F32
    )


def tn(a, b, precision=None):
    return lax.dot_general(
        a, b, (((0,), (0,)), ((), ())), precision=precision, preferred_element_type=F32
    )


def kernel(
    act, grads, mask, w_in, w_out, f_out, f_in, query, out,
    act_v, grads_v, mask_v, w_in_v, w_out_v, f_out_v, f_in_v, query_v,
    f_rows, parts, x_got, near_got, three_got, four_got, two_got,
    q_mine, q_all, q_high, q_low, c_send, c_got,
    load_sem, x_send, x_recv, z_send, z_recv, q_send, q_recv, column_send, column_recv,
    c_send_sem, c_recv_sem, here,
):
    dp = lax.axis_index("dp")
    me = lax.axis_index("tensor")
    qi = lax.axis_index("query")
    z, a = me // 2, lax.rem(me, 2)
    x_lo, core = qi // 2, lax.rem(qi, 2)

    def tensor_peer(k):
        return {"tensor": lax.rem(me + k, 16)}

    def dp_peer(k):
        return {"dp": lax.rem(dp + k, 4)}

    def z_peer(k):
        return {"tensor": lax.rem(z + k + 8, 8) * 2 + a}

    lo_peer = {"query": (1 - x_lo) * 2 + core}
    core_peer = {"query": x_lo * 2 + 1 - core}
    x_peer = {"tensor": z * 2 + 1 - a}

    barrier = pltpu.get_barrier_semaphore()
    peers = [x_peer] + [z_peer(k) for k in (1, -1, 2, -2)] + [lo_peer]
    peers += [dp_peer(k) for k in (1, 2, 3)]
    for peer in peers:
        pl.semaphore_signal(barrier, inc=1, device_id=peer, device_id_type=MESH)


    def load(src, dst, n):
        copy = pltpu.make_async_copy(src, dst, load_sem.at[n])
        copy.start()
        return copy

    load_w_in = load(w_in, w_in_v, 0)
    load_w_out = load(w_out, w_out_v, 1)
    load_rows = []
    for n, k in enumerate(ORDER):
        owner = lax.rem(z + k + 8, 8)
        rows = pl.ds(pl.multiple_of(owner * 256, 256), 256)
        load_rows.append(
            (
                load(act.at[rows], act_v.at[n], 7 + 2 * n),
                load(grads.at[rows], grads_v.at[n], 8 + 2 * n),
            )
        )
        if n == 0:
            load_query = load(query, query_v, 2)
    load_mask = load(mask, mask_v, 3)
    load_f_out = load(f_out, f_out_v, 4)
    load_f_in = load(f_in, f_in_v, 5)

    started = []

    def remote(src, dst, send, recv, peer):
        copy = pltpu.make_async_remote_copy(
            src_ref=src, dst_ref=dst, send_sem=send, recv_sem=recv, device_id=peer, device_id_type=MESH
        )
        copy.start()
        started.append(copy)
        return copy

    def project(k):
        n = ORDER.index(k)
        for copy in load_rows[n]:
            copy.wait()
        p_in = nt(w_in_v[...], act_v[n])
        p_out = nt(w_out_v[...], grads_v[n])
        for half in range(2):
            lanes = slice(128 * half, 128 * half + 128)
            parts[2 * n + half, 0:64, :] = p_in[:, lanes]
            parts[2 * n + half, 64:128, :] = p_out[:, lanes]

    def mine(k):
        return 2 * ORDER.index(k) + a

    def other(k):
        return 2 * ORDER.index(k) + 1 - a

    x_copies = {}

    def send_x(k):
        n = ORDER.index(k)
        x_copies[k] = remote(parts.at[other(k)], x_got.at[n], x_send.at[n], x_recv.at[n], x_peer)

    def add_x(k):
        x_copies[k].wait_recv()
        parts[mine(k)] = parts[mine(k)] + x_got[ORDER.index(k)]

    def send_z(n, src, dst, k):
        return remote(src, dst, z_send.at[n], z_recv.at[n], z_peer(k))

    def column_copy(j, source, owner):
        return pltpu.make_async_remote_copy(
            src_ref=q_mine.at[j], dst_ref=q_all.at[source, x_lo, core],
            send_sem=column_send.at[j], recv_sem=column_recv.at[source],
            device_id={"tensor": owner}, device_id_type=MESH,
        )

    def send_column(j):
        owner = dp * 4 + j

        @pl.when(owner == me)
        def _():
            q_all[me, x_lo, core] = q_mine[j]

        @pl.when(owner != me)
        def _():
            column_copy(j, me, owner).start()

    owns = me // 4 == dp
    my_rows = q_all.at[:, x_lo, core]

    def rows_copy(n, peer):
        return pltpu.make_async_remote_copy(
            src_ref=my_rows, dst_ref=my_rows, send_sem=q_send.at[n], recv_sem=q_recv.at[0],
            device_id=peer, device_id_type=MESH,
        )

    load_w_in.wait()
    load_w_out.wait()
    project(4)
    load_query.wait()
    for j in range(4):
        q_mine[j] = query_v[:, j, :]
    pl.semaphore_wait(barrier, len(peers) + core)
    send_x(4)

    @pl.when(core == 0)
    def _():
        pl.semaphore_signal(barrier, inc=1, device_id=core_peer, device_id_type=MESH)

    pl.semaphore_signal(here.at[0], inc=1, device_id=x_peer, device_id_type=MESH)
    project(3)
    send_x(3)
    project(1)
    pl.semaphore_wait(here.at[0], 1)
    pl.semaphore_signal(here.at[1], inc=1, device_id=z_peer(2), device_id_type=MESH)
    pl.semaphore_signal(here.at[2], inc=1, device_id=z_peer(-2), device_id_type=MESH)
    near_up = send_z(0, parts.at[other(1)], near_got.at[0, 1 - a], 1)
    project(-3)
    send_x(-3)
    project(-1)
    near_down = send_z(1, parts.at[other(-1)], near_got.at[1, 1 - a], -1)
    pl.semaphore_wait(here.at[1], 1)
    pl.semaphore_wait(here.at[2], 1)
    for j in range(4):
        send_column(j)
    add_x(4)
    four_up = send_z(2, parts.at[mine(4), 0:64], four_got.at[0], 2)
    four_down = send_z(3, parts.at[mine(4), 64:128], four_got.at[1], -2)
    project(2)
    send_x(2)
    project(-2)
    send_x(-2)
    project(0)
    add_x(3)
    three_up = send_z(4, parts.at[mine(3)], three_got.at[0], 1)
    near_up.wait_recv()
    near_down.wait_recv()
    parts[other(0)] = parts[other(0)] + near_got[0, 1 - a] + near_got[1, 1 - a]
    send_x(0)
    add_x(-3)
    three_down = send_z(5, parts.at[mine(-3)], three_got.at[1], -1)
    own_up = send_z(8, parts.at[mine(1)], near_got.at[0, a], 1)
    own_down = send_z(9, parts.at[mine(-1)], near_got.at[1, a], -1)

    @pl.when(owns)
    def _():
        for k in range(1, 16):
            source = lax.rem(me + k, 16)
            column_copy(0, source, source).wait_recv()
        for k in (1, 2, 3):
            rows_copy(k, dp_peer(k)).start()

    add_x(2)
    three_up.wait_recv()
    four_up.wait_recv()
    n = mine(2)
    parts[n, 0:64] = parts[n, 0:64] + three_got[0, 0:64] + four_got[0]
    parts[n, 64:128] = parts[n, 64:128] + three_got[0, 64:128]
    two_up = send_z(6, parts.at[n], two_got.at[0], 2)
    add_x(-2)
    three_down.wait_recv()
    four_down.wait_recv()
    n = mine(-2)
    parts[n, 0:64] = parts[n, 0:64] + three_got[1, 0:64]
    parts[n, 64:128] = parts[n, 64:128] + three_got[1, 64:128] + four_got[1]
    two_down = send_z(7, parts.at[n], two_got.at[1], -2)
    own_up.wait_recv()
    own_down.wait_recv()
    total = parts[mine(0)] + near_got[0, a] + near_got[1, a]
    load_mask.wait()
    load_f_out.wait()
    load_f_in.wait()
    for i in range(4):
        f_rows[16 * i : 16 * i + 16, :] = f_out_v[pl.ds(i, 16, stride=4), :]
    weights = jnp.zeros((1, 128), F32)
    for n in range(16):
        piece = mask_v[n // 4 : n // 4 + 1, 128 * (n % 4) : 128 * (n % 4) + 128].astype(F32)
        weights = jnp.where(me == n, piece / 512.0, weights)

    x_copies[0].wait_recv()
    total = total + x_got[ORDER.index(0)]
    two_up.wait_recv()
    total = total + two_got[0]
    two_down.wait_recv()
    total = total + two_got[1]

    side_out = jnp.dot(f_rows[...], total[64:128] * weights, precision=HIGH, preferred_element_type=F32)
    side_in = tn(f_in_v[...], total[0:64], HIGH)
    conditioned = nt(side_out, side_in, HIGH)

    for i in range(4):
        c_send[:, 64 * i : 64 * i + 64] = conditioned[16 * i : 16 * i + 16]
    far_first = sorted(range(1, 16), key=lambda k: -min(k // 2, 8 - k // 2))
    c_copies = [
        remote(c_send, c_got.at[me], c_send_sem.at[k - 1], c_recv_sem.at[k - 1], tensor_peer(k))
        for k in far_first
    ]
    c_got[me] = c_send[...]


    @pl.when(jnp.logical_not(owns))
    def _():
        rows_copy(1, dp_peer(1)).wait_recv()

    lo_copy = remote(my_rows, my_rows, q_send.at[4], q_recv.at[1], lo_peer)
    lo_copy.wait_recv()
    block = q_all.at[:, :, core]
    core_copy = pltpu.make_async_remote_copy(
        src_ref=block, dst_ref=block, send_sem=q_send.at[5], recv_sem=q_recv.at[2],
        device_id=core_peer, device_id_type=MESH,
    )
    started.append(core_copy)

    @pl.when(core == 1)
    def _():
        core_copy.start()

    core_copy.wait_recv()

    @pl.when(core == 0)
    def _():
        core_copy.start()

    q = q_all[...].reshape(512, 256)
    high = q.astype(jnp.bfloat16)
    q_high[...] = high
    q_low[...] = (q - high.astype(F32)).astype(jnp.bfloat16)

    for copy in c_copies[::-1]:
        copy.wait_recv()
    got = c_got[...].reshape(4, 4, 16, 256)
    got = (got[:, 0] + got[:, 1] + got[:, 2] + got[:, 3]).reshape(64, 256)
    high = got.astype(jnp.bfloat16)
    low = (got - high.astype(F32)).astype(jnp.bfloat16)
    pairs = nt(high, q_high[...]) + (nt(high, q_low[...]) + nt(low, q_high[...]))
    left = lax.rem(lax.broadcasted_iota(jnp.int32, (64, 512), 0), 16)
    right = lax.broadcasted_iota(jnp.int32, (64, 512), 1) // 32
    pairs = jnp.where(left == right, pairs, 0.0).reshape(4, 16, 512)
    scores = jnp.sum(pairs, axis=1)
    scores = scores[:, 0:128] + scores[:, 128:256] + scores[:, 256:384] + scores[:, 384:512]
    out[...] = scores[:, 0:32] + scores[:, 32:64] + scores[:, 64:96] + scores[:, 96:128]

    for j in range(4):

        @pl.when(dp * 4 + j != me)
        def _():
            column_copy(j, me, dp * 4 + j).wait_send()

    @pl.when(owns)
    def _():
        for k in (1, 2, 3):
            rows_copy(k, dp_peer(k)).wait_send()

    for copy in started:
        copy.wait_send()


def local(act, grads, mask, w_in, w_out, f_out, f_in, query):
    docs, length, hidden = act.shape
    model = grads.shape[2]
    vmem, sem = pltpu.VMEM, pltpu.SemaphoreType.DMA
    scores = pl.pallas_call(
        kernel,
        name="influence",
        out_shape=jax.ShapeDtypeStruct((4, 32), F32),
        in_specs=[pl.BlockSpec(memory_space=pl.ANY)] * 8,
        out_specs=pl.BlockSpec(memory_space=pltpu.VMEM),
        scratch_shapes=[
            vmem((8, 256, hidden), jnp.bfloat16),
            vmem((8, 256, model), jnp.bfloat16),
            vmem((4, 512), jnp.int32),
            vmem((64, hidden), jnp.bfloat16),
            vmem((64, model), jnp.bfloat16),
            vmem((64, 64), F32),
            vmem((64, 64), F32),
            vmem((8, 4, 256), F32),
            vmem((64, 64), F32),
            vmem((16, 128, 128), F32),
            vmem((8, 128, 128), F32),
            vmem((2, 2, 128, 128), F32),
            vmem((2, 128, 128), F32),
            vmem((2, 64, 128), F32),
            vmem((2, 128, 128), F32),
            vmem((4, 8, 256), F32),
            vmem((16, 2, 2, 8, 256), F32),
            vmem((512, 256), jnp.bfloat16),
            vmem((512, 256), jnp.bfloat16),
            vmem((16, 256), F32),
            vmem((16, 16, 256), F32),
            sem((23,)),
            sem((8,)), sem((8,)),
            sem((10,)), sem((10,)),
            sem((6,)), sem((3,)),
            sem((4,)), sem((16,)),
            sem((15,)), sem((15,)),
            pltpu.SemaphoreType.REGULAR((3,)),
        ],
        compiler_params=pltpu.CompilerParams(
            collective_id=0, has_side_effects=True, vmem_limit_bytes=56 * 2**20
        ),
    )(
        act.reshape(docs * length, hidden),
        grads.reshape(docs * length, model),
        mask, w_in.T, w_out.T, f_out, f_in, query,
    )
    return scores.reshape(4, 32, 1)


def solution(mesh):
    placed = (
        P(("dp", "query"), None, "tensor"),
        P(("dp", "query"), None, "tensor"),
        P(("dp", "query"), None),
        P("tensor", None),
        P("tensor", None),
        P(),
        P(),
        P("query", "dp", "tensor"),
    )
    return jax.shard_map(
        local,
        mesh=mesh,
        in_specs=placed,
        out_specs=P(("dp", "query"), None, "tensor"),
        check_vma=False,
    )
```

```python
import functools

import jax
import jax.numpy as jnp
from jax import lax
from jax.experimental import pallas as pl
from jax.experimental.pallas import tpu as pltpu
from jax.sharding import PartitionSpec as P

MESH = pl.DeviceIdType.MESH
F32 = jnp.float32
HIGH = lax.Precision.HIGHEST
ORDER = (4, 1, 3, -1, -3, 2, -2, 0)


def nt(a, b, precision=None):
    return lax.dot_general(
        a, b, (((1,), (1,)), ((), ())), precision=precision, preferred_element_type=F32
    )


def tn(a, b, precision=None):
    return lax.dot_general(
        a, b, (((0,), (0,)), ((), ())), precision=precision, preferred_element_type=F32
    )


def kernel(
    act, grads, mask, w_in, w_out, f_out, f_in, query, out,
    act_v, grads_v, mask_v, w_in_v, w_out_v, f_out_v, f_in_v, query_v,
    f_rows, parts, x_got, near_got, three_got, four_got, two_got,
    q_mine, q_all, q_high, q_low, c_send, c_got,
    load_sem, x_send, x_recv, z_send, z_recv, q_send, q_recv, column_send, column_recv,
    c_send_sem, c_recv_sem, here,
):
    dp = lax.axis_index("dp")
    me = lax.axis_index("tensor")
    qi = lax.axis_index("query")
    z, a = me // 2, lax.rem(me, 2)
    x_lo, core = qi // 2, lax.rem(qi, 2)

    def tensor_peer(k):
        return {"tensor": lax.rem(me + k, 16)}

    def dp_peer(k):
        return {"dp": lax.rem(dp + k, 4)}

    def z_peer(k):
        return {"tensor": lax.rem(z + k + 8, 8) * 2 + a}

    lo_peer = {"query": (1 - x_lo) * 2 + core}
    core_peer = {"query": x_lo * 2 + 1 - core}
    x_peer = {"tensor": z * 2 + 1 - a}

    barrier = pltpu.get_barrier_semaphore()
    peers = [x_peer] + [z_peer(k) for k in (1, -1, 2, -2)] + [lo_peer]
    peers += [dp_peer(k) for k in (1, 2, 3)]
    for peer in peers:
        pl.semaphore_signal(barrier, inc=1, device_id=peer, device_id_type=MESH)


    def load(src, dst, n):
        copy = pltpu.make_async_copy(src, dst, load_sem.at[n])
        copy.start()
        return copy

    load_w_in = load(w_in, w_in_v, 0)
    load_w_out = load(w_out, w_out_v, 1)
    load_rows = []
    for n, k in enumerate(ORDER):
        owner = lax.rem(z + k + 8, 8)
        rows = pl.ds(pl.multiple_of(owner * 256, 256), 256)
        load_rows.append(
            (
                load(act.at[rows], act_v.at[n], 7 + 2 * n),
                load(grads.at[rows], grads_v.at[n], 8 + 2 * n),
            )
        )
        if n == 0:
            load_query = load(query, query_v, 2)
    load_mask = load(mask, mask_v, 3)
    load_f_out = load(f_out, f_out_v, 4)
    load_f_in = load(f_in, f_in_v, 5)

    started = []

    def remote(src, dst, send, recv, peer):
        copy = pltpu.make_async_remote_copy(
            src_ref=src, dst_ref=dst, send_sem=send, recv_sem=recv, device_id=peer, device_id_type=MESH
        )
        copy.start()
        started.append(copy)
        return copy

    def project(k):
        n = ORDER.index(k)
        for copy in load_rows[n]:
            copy.wait()
        p_in = nt(w_in_v[...], act_v[n])
        p_out = nt(w_out_v[...], grads_v[n])
        for half in range(2):
            lanes = slice(128 * half, 128 * half + 128)
            parts[2 * n + half, 0:64, :] = p_in[:, lanes]
            parts[2 * n + half, 64:128, :] = p_out[:, lanes]

    def mine(k):
        return 2 * ORDER.index(k) + a

    def other(k):
        return 2 * ORDER.index(k) + 1 - a

    x_copies = {}

    def send_x(k):
        n = ORDER.index(k)
        x_copies[k] = remote(parts.at[other(k)], x_got.at[n], x_send.at[n], x_recv.at[n], x_peer)

    def add_x(k):
        x_copies[k].wait_recv()
        parts[mine(k)] = parts[mine(k)] + x_got[ORDER.index(k)]

    def send_z(n, src, dst, k):
        return remote(src, dst, z_send.at[n], z_recv.at[n], z_peer(k))

    def column_copy(j, source, owner):
        return pltpu.make_async_remote_copy(
            src_ref=q_mine.at[j], dst_ref=q_all.at[source, x_lo, core],
            send_sem=column_send.at[j], recv_sem=column_recv.at[source],
            device_id={"tensor": owner}, device_id_type=MESH,
        )

    def send_column(j):
        owner = dp * 4 + j

        @pl.when(owner == me)
        def _():
            q_all[me, x_lo, core] = q_mine[j]

        @pl.when(owner != me)
        def _():
            column_copy(j, me, owner).start()

    owns = me // 4 == dp
    my_rows = q_all.at[:, x_lo, core]

    def rows_copy(n, peer):
        return pltpu.make_async_remote_copy(
            src_ref=my_rows, dst_ref=my_rows, send_sem=q_send.at[n], recv_sem=q_recv.at[0],
            device_id=peer, device_id_type=MESH,
        )

    load_w_in.wait()
    load_w_out.wait()
    project(4)
    pl.semaphore_wait(barrier, len(peers) + core)
    send_x(4)

    @pl.when(core == 0)
    def _():
        pl.semaphore_signal(barrier, inc=1, device_id=core_peer, device_id_type=MESH)

    pl.semaphore_signal(here.at[0], inc=1, device_id=x_peer, device_id_type=MESH)
    load_query.wait()
    for j in range(4):
        q_mine[j] = query_v[:, j, :]
    project(1)
    near_up = send_z(0, parts.at[other(1)], near_got.at[0, 1 - a], 1)
    project(3)
    send_x(3)
    pl.semaphore_wait(here.at[0], 1)
    pl.semaphore_signal(here.at[1], inc=1, device_id=z_peer(2), device_id_type=MESH)
    pl.semaphore_signal(here.at[2], inc=1, device_id=z_peer(-2), device_id_type=MESH)
    project(-1)
    near_down = send_z(1, parts.at[other(-1)], near_got.at[1, 1 - a], -1)
    project(-3)
    send_x(-3)
    pl.semaphore_wait(here.at[1], 1)
    pl.semaphore_wait(here.at[2], 1)
    for j in range(4):
        send_column(j)
    add_x(4)
    four_up = send_z(2, parts.at[mine(4), 0:64], four_got.at[0], 2)
    four_down = send_z(3, parts.at[mine(4), 64:128], four_got.at[1], -2)
    project(2)
    send_x(2)
    project(-2)
    send_x(-2)
    project(0)
    near_up.wait_recv()
    near_down.wait_recv()
    parts[other(0)] = parts[other(0)] + near_got[0, 1 - a] + near_got[1, 1 - a]
    send_x(0)
    add_x(3)
    three_up = send_z(4, parts.at[mine(3)], three_got.at[0], 1)
    add_x(-3)
    three_down = send_z(5, parts.at[mine(-3)], three_got.at[1], -1)
    own_up = send_z(8, parts.at[mine(1)], near_got.at[0, a], 1)
    own_down = send_z(9, parts.at[mine(-1)], near_got.at[1, a], -1)

    @pl.when(owns)
    def _():
        for k in range(1, 16):
            source = lax.rem(me + k, 16)
            column_copy(0, source, source).wait_recv()
        for k in (1, 2, 3):
            rows_copy(k, dp_peer(k)).start()

    add_x(2)
    three_up.wait_recv()
    four_up.wait_recv()
    n = mine(2)
    parts[n, 0:64] = parts[n, 0:64] + three_got[0, 0:64] + four_got[0]
    parts[n, 64:128] = parts[n, 64:128] + three_got[0, 64:128]
    two_up = send_z(6, parts.at[n], two_got.at[0], 2)
    add_x(-2)
    three_down.wait_recv()
    four_down.wait_recv()
    n = mine(-2)
    parts[n, 0:64] = parts[n, 0:64] + three_got[1, 0:64]
    parts[n, 64:128] = parts[n, 64:128] + three_got[1, 64:128] + four_got[1]
    two_down = send_z(7, parts.at[n], two_got.at[1], -2)
    own_up.wait_recv()
    own_down.wait_recv()
    total = parts[mine(0)] + near_got[0, a] + near_got[1, a]
    load_mask.wait()
    load_f_out.wait()
    load_f_in.wait()
    for i in range(4):
        f_rows[16 * i : 16 * i + 16, :] = f_out_v[pl.ds(i, 16, stride=4), :]
    weights = jnp.zeros((1, 128), F32)
    for n in range(16):
        piece = mask_v[n // 4 : n // 4 + 1, 128 * (n % 4) : 128 * (n % 4) + 128].astype(F32)
        weights = jnp.where(me == n, piece / 512.0, weights)

    x_copies[0].wait_recv()
    total = total + x_got[ORDER.index(0)]
    two_up.wait_recv()
    total = total + two_got[0]
    two_down.wait_recv()
    total = total + two_got[1]

    side_out = jnp.dot(f_rows[...], total[64:128] * weights, precision=HIGH, preferred_element_type=F32)
    side_in = tn(f_in_v[...], total[0:64], HIGH)
    conditioned = nt(side_out, side_in, HIGH)

    for i in range(4):
        c_send[:, 64 * i : 64 * i + 64] = conditioned[16 * i : 16 * i + 16]
    far_first = sorted(range(1, 16), key=lambda k: -min(k // 2, 8 - k // 2))
    c_copies = [
        remote(c_send, c_got.at[me], c_send_sem.at[k - 1], c_recv_sem.at[k - 1], tensor_peer(k))
        for k in far_first
    ]
    c_got[me] = c_send[...]


    @pl.when(jnp.logical_not(owns))
    def _():
        rows_copy(1, dp_peer(1)).wait_recv()

    lo_copy = remote(my_rows, my_rows, q_send.at[4], q_recv.at[1], lo_peer)
    lo_copy.wait_recv()
    block = q_all.at[:, :, core]
    core_copy = pltpu.make_async_remote_copy(
        src_ref=block, dst_ref=block, send_sem=q_send.at[5], recv_sem=q_recv.at[2],
        device_id=core_peer, device_id_type=MESH,
    )
    started.append(core_copy)

    @pl.when(core == 1)
    def _():
        core_copy.start()

    core_copy.wait_recv()

    @pl.when(core == 0)
    def _():
        core_copy.start()

    q = q_all[...].reshape(512, 256)
    high = q.astype(jnp.bfloat16)
    q_high[...] = high
    q_low[...] = (q - high.astype(F32)).astype(jnp.bfloat16)

    for j in range(4):

        @pl.when(dp * 4 + j != me)
        def _():
            column_copy(j, me, dp * 4 + j).wait_send()

    @pl.when(owns)
    def _():
        for k in (1, 2, 3):
            rows_copy(k, dp_peer(k)).wait_send()

    for copy in started:
        copy.wait_send()

    for copy in c_copies[::-1]:
        copy.wait_recv()
    got = c_got[...].reshape(4, 4, 16, 256)
    got = (got[:, 0] + got[:, 1] + got[:, 2] + got[:, 3]).reshape(64, 256)
    high = got.astype(jnp.bfloat16)
    low = (got - high.astype(F32)).astype(jnp.bfloat16)
    pairs = nt(high, q_high[...]) + (nt(high, q_low[...]) + nt(low, q_high[...]))
    left = lax.rem(lax.broadcasted_iota(jnp.int32, (64, 512), 0), 16)
    right = lax.broadcasted_iota(jnp.int32, (64, 512), 1) // 32
    pairs = jnp.where(left == right, pairs, 0.0).reshape(4, 16, 512)
    scores = jnp.sum(pairs, axis=1)
    scores = scores[:, 0:128] + scores[:, 128:256] + scores[:, 256:384] + scores[:, 384:512]
    out[...] = scores[:, 0:32] + scores[:, 32:64] + scores[:, 64:96] + scores[:, 96:128]


def local(act, grads, mask, w_in, w_out, f_out, f_in, query):
    docs, length, hidden = act.shape
    model = grads.shape[2]
    vmem, sem = pltpu.VMEM, pltpu.SemaphoreType.DMA
    scores = pl.pallas_call(
        kernel,
        name="influence",
        out_shape=jax.ShapeDtypeStruct((4, 32), F32),
        in_specs=[pl.BlockSpec(memory_space=pl.ANY)] * 8,
        out_specs=pl.BlockSpec(memory_space=pltpu.VMEM),
        scratch_shapes=[
            vmem((8, 256, hidden), jnp.bfloat16),
            vmem((8, 256, model), jnp.bfloat16),
            vmem((4, 512), jnp.int32),
            vmem((64, hidden), jnp.bfloat16),
            vmem((64, model), jnp.bfloat16),
            vmem((64, 64), F32),
            vmem((64, 64), F32),
            vmem((8, 4, 256), F32),
            vmem((64, 64), F32),
            vmem((16, 128, 128), F32),
            vmem((8, 128, 128), F32),
            vmem((2, 2, 128, 128), F32),
            vmem((2, 128, 128), F32),
            vmem((2, 64, 128), F32),
            vmem((2, 128, 128), F32),
            vmem((4, 8, 256), F32),
            vmem((16, 2, 2, 8, 256), F32),
            vmem((512, 256), jnp.bfloat16),
            vmem((512, 256), jnp.bfloat16),
            vmem((16, 256), F32),
            vmem((16, 16, 256), F32),
            sem((23,)),
            sem((8,)), sem((8,)),
            sem((10,)), sem((10,)),
            sem((6,)), sem((3,)),
            sem((4,)), sem((16,)),
            sem((15,)), sem((15,)),
            pltpu.SemaphoreType.REGULAR((3,)),
        ],
        compiler_params=pltpu.CompilerParams(
            collective_id=0, has_side_effects=True, vmem_limit_bytes=56549376
        ),
    )(
        act.reshape(docs * length, hidden),
        grads.reshape(docs * length, model),
        mask, w_in.T, w_out.T, f_out, f_in, query,
    )
    return scores.reshape(4, 32, 1)


def solution(mesh):
    placed = (
        P(("dp", "query"), None, "tensor"),
        P(("dp", "query"), None, "tensor"),
        P(("dp", "query"), None),
        P("tensor", None),
        P("tensor", None),
        P(),
        P(),
        P("query", "dp", "tensor"),
    )
    return jax.shard_map(
        local,
        mesh=mesh,
        in_specs=placed,
        out_specs=P(("dp", "query"), None, "tensor"),
        check_vma=False,
    )
```

```python
import functools

import jax
import jax.numpy as jnp
from jax import lax
from jax.experimental import pallas as pl
from jax.experimental.pallas import tpu as pltpu
from jax.sharding import PartitionSpec as P

MESH = pl.DeviceIdType.MESH
F32 = jnp.float32
HIGH = lax.Precision.HIGHEST
ORDER = (4, 1, 3, -1, -3, 2, -2, 0)


def nt(a, b, precision=None):
    return lax.dot_general(
        a, b, (((1,), (1,)), ((), ())), precision=precision, preferred_element_type=F32
    )


def tn(a, b, precision=None):
    return lax.dot_general(
        a, b, (((0,), (0,)), ((), ())), precision=precision, preferred_element_type=F32
    )


def kernel(
    act, grads, mask, w_in, w_out, f_out, f_in, query, out,
    act_v, grads_v, mask_v, w_in_v, w_out_v, f_out_v, f_in_v, query_v,
    f_rows, parts, x_got, near_got, three_got, four_got, two_got,
    q_mine, q_all, q_high, q_low, c_send, c_got,
    load_sem, x_send, x_recv, z_send, z_recv, q_send, q_recv, column_send, column_recv,
    c_send_sem, c_recv_sem, here,
):
    dp = lax.axis_index("dp")
    me = lax.axis_index("tensor")
    qi = lax.axis_index("query")
    z, a = me // 2, lax.rem(me, 2)
    x_lo, core = qi // 2, lax.rem(qi, 2)

    def dp_peer(k):
        return {"dp": lax.rem(dp + k, 4)}

    def z_peer(k):
        return {"tensor": lax.rem(z + k + 8, 8) * 2 + a}

    lo_peer = {"query": (1 - x_lo) * 2 + core}
    core_peer = {"query": x_lo * 2 + 1 - core}
    x_peer = {"tensor": z * 2 + 1 - a}

    barrier = pltpu.get_barrier_semaphore()
    peers = [x_peer] + [z_peer(k) for k in (2, -2)] + [dp_peer(k) for k in (2, 1, 3)]
    peers += [z_peer(k) for k in (1, -1)] + [lo_peer]
    for peer in peers:
        pl.semaphore_signal(barrier, inc=1, device_id=peer, device_id_type=MESH)


    def load(src, dst, n):
        copy = pltpu.make_async_copy(src, dst, load_sem.at[n])
        copy.start(priority=1)
        return copy

    load_w_in = load(w_in, w_in_v, 0)
    load_w_out = load(w_out, w_out_v, 1)
    load_rows = []
    for n, k in enumerate(ORDER):
        owner = lax.rem(z + k + 8, 8)
        rows = pl.ds(pl.multiple_of(owner * 256, 256), 256)
        load_rows.append(
            (
                load(act.at[rows], act_v.at[n], 7 + 2 * n),
                load(grads.at[rows], grads_v.at[n], 8 + 2 * n),
            )
        )
        if n == 0:
            load_query = load(query, query_v, 2)
    load_mask = load(mask, mask_v, 3)
    load_f_out = load(f_out, f_out_v, 4)
    load_f_in = load(f_in, f_in_v, 5)

    started = []

    def remote(src, dst, send, recv, peer):
        copy = pltpu.make_async_remote_copy(
            src_ref=src, dst_ref=dst, send_sem=send, recv_sem=recv, device_id=peer, device_id_type=MESH
        )
        copy.start()
        started.append(copy)
        return copy

    def project(k):
        n = ORDER.index(k)
        for copy in load_rows[n]:
            copy.wait()
        p_in = nt(w_in_v[...], act_v[n])
        p_out = nt(w_out_v[...], grads_v[n])
        for half in range(2):
            lanes = slice(128 * half, 128 * half + 128)
            parts[2 * n + half, 0:64, :] = p_in[:, lanes]
            parts[2 * n + half, 64:128, :] = p_out[:, lanes]

    def mine(k):
        return 2 * ORDER.index(k) + a

    def other(k):
        return 2 * ORDER.index(k) + 1 - a

    x_copies = {}

    def send_x(k):
        n = ORDER.index(k)
        x_copies[k] = remote(parts.at[other(k)], x_got.at[n], x_send.at[n], x_recv.at[n], x_peer)

    def add_x(k):
        x_copies[k].wait_recv()
        parts[mine(k)] = parts[mine(k)] + x_got[ORDER.index(k)]

    def send_z(n, src, dst, k):
        return remote(src, dst, z_send.at[n], z_recv.at[n], z_peer(k))

    def column_copy(j, source, owner):
        return pltpu.make_async_remote_copy(
            src_ref=q_mine.at[j], dst_ref=q_all.at[source, x_lo, core],
            send_sem=column_send.at[j], recv_sem=column_recv.at[source],
            device_id={"tensor": owner}, device_id_type=MESH,
        )

    def send_column(j):
        owner = dp * 4 + j

        @pl.when(owner == me)
        def _():
            q_all[me, x_lo, core] = q_mine[j]

        @pl.when(owner != me)
        def _():
            column_copy(j, me, owner).start()

    owns = me // 4 == dp
    my_rows = q_all.at[:, x_lo, core]

    def rows_copy(n, peer):
        return pltpu.make_async_remote_copy(
            src_ref=my_rows, dst_ref=my_rows, send_sem=q_send.at[n], recv_sem=q_recv.at[0],
            device_id=peer, device_id_type=MESH,
        )

    load_w_in.wait()
    load_w_out.wait()
    project(4)
    pl.semaphore_wait(barrier, len(peers) + core)
    send_x(4)

    @pl.when(core == 0)
    def _():
        pl.semaphore_signal(barrier, inc=1, device_id=core_peer, device_id_type=MESH)

    pl.semaphore_signal(here.at[0], inc=1, device_id=x_peer, device_id_type=MESH)
    load_query.wait()
    for j in range(4):
        q_mine[j] = query_v[:, j, :]
    project(1)
    near_up = send_z(0, parts.at[other(1)], near_got.at[0, 1 - a], 1)
    project(3)
    send_x(3)
    pl.semaphore_wait(here.at[0], 1)
    pl.semaphore_signal(here.at[1], inc=1, device_id=z_peer(2), device_id_type=MESH)
    pl.semaphore_signal(here.at[2], inc=1, device_id=z_peer(-2), device_id_type=MESH)
    project(-1)
    near_down = send_z(1, parts.at[other(-1)], near_got.at[1, 1 - a], -1)
    project(-3)
    send_x(-3)
    pl.semaphore_wait(here.at[1], 1)
    pl.semaphore_wait(here.at[2], 1)
    for j in range(4):
        send_column(j)
    add_x(4)
    four_up = send_z(2, parts.at[mine(4), 0:64], four_got.at[0], 2)
    four_down = send_z(3, parts.at[mine(4), 64:128], four_got.at[1], -2)
    project(2)
    send_x(2)
    project(-2)
    send_x(-2)
    project(0)
    near_up.wait_recv()
    near_down.wait_recv()
    parts[other(0)] = parts[other(0)] + near_got[0, 1 - a] + near_got[1, 1 - a]
    send_x(0)
    add_x(3)
    three_up = send_z(4, parts.at[mine(3)], three_got.at[0], 1)
    add_x(-3)
    three_down = send_z(5, parts.at[mine(-3)], three_got.at[1], -1)
    own_up = send_z(8, parts.at[mine(1)], near_got.at[0, a], 1)
    own_down = send_z(9, parts.at[mine(-1)], near_got.at[1, a], -1)

    @pl.when(owns)
    def _():
        for k in range(1, 16):
            source = lax.rem(me + k, 16)
            column_copy(0, source, source).wait_recv()
        for k in (1, 2, 3):
            rows_copy(k, dp_peer(k)).start()

    add_x(2)
    three_up.wait_recv()
    four_up.wait_recv()
    n = mine(2)
    parts[n, 0:64] = parts[n, 0:64] + three_got[0, 0:64] + four_got[0]
    parts[n, 64:128] = parts[n, 64:128] + three_got[0, 64:128]
    two_up = send_z(6, parts.at[n], two_got.at[0], 2)
    add_x(-2)
    three_down.wait_recv()
    four_down.wait_recv()
    n = mine(-2)
    parts[n, 0:64] = parts[n, 0:64] + three_got[1, 0:64]
    parts[n, 64:128] = parts[n, 64:128] + three_got[1, 64:128] + four_got[1]
    two_down = send_z(7, parts.at[n], two_got.at[1], -2)
    own_up.wait_recv()
    own_down.wait_recv()
    total = parts[mine(0)] + near_got[0, a] + near_got[1, a]
    load_mask.wait()
    load_f_out.wait()
    load_f_in.wait()
    for i in range(4):
        f_rows[16 * i : 16 * i + 16, :] = f_out_v[pl.ds(i, 16, stride=4), :]
    weights = jnp.zeros((1, 128), F32)
    for n in range(16):
        piece = mask_v[n // 4 : n // 4 + 1, 128 * (n % 4) : 128 * (n % 4) + 128].astype(F32)
        weights = jnp.where(me == n, piece / 512.0, weights)

    x_copies[0].wait_recv()
    total = total + x_got[ORDER.index(0)]
    two_up.wait_recv()
    total = total + two_got[0]
    two_down.wait_recv()
    total = total + two_got[1]

    side_out = jnp.dot(f_rows[...], total[64:128] * weights, precision=HIGH, preferred_element_type=F32)
    side_in = tn(f_in_v[...], total[0:64], HIGH)
    conditioned = nt(side_out, side_in, HIGH)

    for i in range(4):
        c_send[:, 64 * i : 64 * i + 64] = conditioned[16 * i : 16 * i + 16]
    far_first = [(k, row) for k in (4, 3, -3, 2, -2, 1, -1, 0) for row in (0, 1) if (k, row) != (0, 0)]
    c_copies = []
    for n, (k, row) in enumerate(far_first):
        peer = lax.rem(z + k + 8, 8) * 2 + (1 - a if row else a)
        c_copies.append(remote(c_send, c_got.at[me], c_send_sem.at[n], c_recv_sem.at[n], {"tensor": peer}))
    c_got[me] = c_send[...]


    @pl.when(jnp.logical_not(owns))
    def _():
        rows_copy(1, dp_peer(1)).wait_recv()

    lo_copy = remote(my_rows, my_rows, q_send.at[4], q_recv.at[1], lo_peer)
    lo_copy.wait_recv()
    block = q_all.at[:, :, core]
    core_copy = pltpu.make_async_remote_copy(
        src_ref=block, dst_ref=block, send_sem=q_send.at[5], recv_sem=q_recv.at[2],
        device_id=core_peer, device_id_type=MESH,
    )
    started.append(core_copy)

    @pl.when(core == 1)
    def _():
        core_copy.start()

    core_copy.wait_recv()

    @pl.when(core == 0)
    def _():
        core_copy.start()

    q = q_all[...].reshape(512, 256)
    high = q.astype(jnp.bfloat16)
    q_high[...] = high
    q_low[...] = (q - high.astype(F32)).astype(jnp.bfloat16)

    for j in range(4):

        @pl.when(dp * 4 + j != me)
        def _():
            column_copy(j, me, dp * 4 + j).wait_send()

    @pl.when(owns)
    def _():
        for k in (1, 2, 3):
            rows_copy(k, dp_peer(k)).wait_send()

    for copy in started:
        copy.wait_send()

    for copy in c_copies[::-1]:
        copy.wait_recv()
    got = c_got[...].reshape(4, 4, 16, 256)
    got = (got[:, 0] + got[:, 1] + got[:, 2] + got[:, 3]).reshape(64, 256)
    high = got.astype(jnp.bfloat16)
    low = (got - high.astype(F32)).astype(jnp.bfloat16)
    pairs = nt(high, q_high[...]) + (nt(high, q_low[...]) + nt(low, q_high[...]))
    left = lax.rem(lax.broadcasted_iota(jnp.int32, (64, 512), 0), 16)
    right = lax.broadcasted_iota(jnp.int32, (64, 512), 1) // 32
    pairs = jnp.where(left == right, pairs, 0.0).reshape(4, 16, 512)
    scores = jnp.sum(pairs, axis=1)
    scores = scores[:, 0:128] + scores[:, 128:256] + scores[:, 256:384] + scores[:, 384:512]
    out[...] = scores[:, 0:32] + scores[:, 32:64] + scores[:, 64:96] + scores[:, 96:128]


def local(act, grads, mask, w_in, w_out, f_out, f_in, query):
    docs, length, hidden = act.shape
    model = grads.shape[2]
    vmem, sem = pltpu.VMEM, pltpu.SemaphoreType.DMA
    scores = pl.pallas_call(
        kernel,
        name="influence",
        out_shape=jax.ShapeDtypeStruct((4, 32), F32),
        in_specs=[pl.BlockSpec(memory_space=pl.ANY)] * 8,
        out_specs=pl.BlockSpec(memory_space=pltpu.VMEM),
        scratch_shapes=[
            vmem((8, 256, hidden), jnp.bfloat16),
            vmem((8, 256, model), jnp.bfloat16),
            vmem((4, 512), jnp.int32),
            vmem((64, hidden), jnp.bfloat16),
            vmem((64, model), jnp.bfloat16),
            vmem((64, 64), F32),
            vmem((64, 64), F32),
            vmem((8, 4, 256), F32),
            vmem((64, 64), F32),
            vmem((16, 128, 128), F32),
            vmem((8, 128, 128), F32),
            vmem((2, 2, 128, 128), F32),
            vmem((2, 128, 128), F32),
            vmem((2, 64, 128), F32),
            vmem((2, 128, 128), F32),
            vmem((4, 8, 256), F32),
            vmem((16, 2, 2, 8, 256), F32),
            vmem((512, 256), jnp.bfloat16),
            vmem((512, 256), jnp.bfloat16),
            vmem((16, 256), F32),
            vmem((16, 16, 256), F32),
            sem((23,)),
            sem((8,)), sem((8,)),
            sem((10,)), sem((10,)),
            sem((6,)), sem((3,)),
            sem((4,)), sem((16,)),
            sem((15,)), sem((15,)),
            pltpu.SemaphoreType.REGULAR((3,)),
        ],
        compiler_params=pltpu.CompilerParams(
            collective_id=0, has_side_effects=True, vmem_limit_bytes=56549376
        ),
    )(
        act.reshape(docs * length, hidden),
        grads.reshape(docs * length, model),
        mask, w_in.T, w_out.T, f_out, f_in, query,
    )
    return scores.reshape(4, 32, 1)


def solution(mesh):
    placed = (
        P(("dp", "query"), None, "tensor"),
        P(("dp", "query"), None, "tensor"),
        P(("dp", "query"), None),
        P("tensor", None),
        P("tensor", None),
        P(),
        P(),
        P("query", "dp", "tensor"),
    )
    return jax.shard_map(
        local,
        mesh=mesh,
        in_specs=placed,
        out_specs=P(("dp", "query"), None, "tensor"),
        check_vma=False,
    )
```

```python
import functools

import jax
import jax.numpy as jnp
from jax import lax
from jax.experimental import pallas as pl
from jax.experimental.pallas import tpu as pltpu
from jax.sharding import PartitionSpec as P

MESH = pl.DeviceIdType.MESH
F32 = jnp.float32
HIGH = lax.Precision.HIGHEST
ORDER = (4, 1, 3, -1, -3, 2, -2, 0)


def nt(a, b, precision=None):
    return lax.dot_general(
        a, b, (((1,), (1,)), ((), ())), precision=precision, preferred_element_type=F32
    )


def tn(a, b, precision=None):
    return lax.dot_general(
        a, b, (((0,), (0,)), ((), ())), precision=precision, preferred_element_type=F32
    )


def kernel(
    act, grads, mask, w_in, w_out, f_out, f_in, query, out,
    act_v, grads_v, mask_v, w_in_v, w_out_v, f_out_v, f_in_v, query_v,
    f_rows, parts, x_got, near_got, three_got, four_got, two_got,
    q_mine, q_all, q_high, q_low, c_send, c_got,
    load_sem, x_send, x_recv, z_send, z_recv, q_send, q_recv, column_send, column_recv,
    c_send_sem, c_recv_sem, here,
):
    dp = lax.axis_index("dp")
    me = lax.axis_index("tensor")
    qi = lax.axis_index("query")
    z, a = me // 2, lax.rem(me, 2)
    x_lo, core = qi // 2, lax.rem(qi, 2)

    def dp_peer(k):
        return {"dp": lax.rem(dp + k, 4)}

    def z_peer(k):
        return {"tensor": lax.rem(z + k + 8, 8) * 2 + a}

    lo_peer = {"query": (1 - x_lo) * 2 + core}
    core_peer = {"query": x_lo * 2 + 1 - core}
    x_peer = {"tensor": z * 2 + 1 - a}

    barrier = pltpu.get_barrier_semaphore()
    peers = [x_peer] + [z_peer(k) for k in (2, -2)] + [dp_peer(k) for k in (2, 1, 3)]
    peers += [z_peer(k) for k in (1, -1)] + [lo_peer]
    for peer in peers:
        pl.semaphore_signal(barrier, inc=1, device_id=peer, device_id_type=MESH)


    def load(src, dst, n):
        copy = pltpu.make_async_copy(src, dst, load_sem.at[n])
        copy.start(priority=1)
        return copy

    load_w_in = load(w_in, w_in_v, 0)
    load_w_out = load(w_out, w_out_v, 1)
    load_rows = []
    for n, k in enumerate(ORDER):
        owner = lax.rem(z + k + 8, 8)
        rows = pl.ds(pl.multiple_of(owner * 256, 256), 256)
        load_rows.append(
            (
                load(act.at[rows], act_v.at[n], 7 + 2 * n),
                load(grads.at[rows], grads_v.at[n], 8 + 2 * n),
            )
        )
        if n == 0:
            load_query = load(query, query_v, 2)
    load_mask = load(mask, mask_v, 3)
    load_f_out = load(f_out, f_out_v, 4)
    load_f_in = load(f_in, f_in_v, 5)

    started = []

    def remote(src, dst, send, recv, peer):
        copy = pltpu.make_async_remote_copy(
            src_ref=src, dst_ref=dst, send_sem=send, recv_sem=recv, device_id=peer, device_id_type=MESH
        )
        copy.start()
        started.append(copy)
        return copy

    def project(k):
        n = ORDER.index(k)
        for copy in load_rows[n]:
            copy.wait()
        p_in = nt(w_in_v[...], act_v[n])
        p_out = nt(w_out_v[...], grads_v[n])
        for half in range(2):
            lanes = slice(128 * half, 128 * half + 128)
            parts[2 * n + half, 0:64, :] = p_in[:, lanes]
            parts[2 * n + half, 64:128, :] = p_out[:, lanes]

    def mine(k):
        return 2 * ORDER.index(k) + a

    def other(k):
        return 2 * ORDER.index(k) + 1 - a

    x_copies = {}

    def send_x(k):
        n = ORDER.index(k)
        x_copies[k] = remote(parts.at[other(k)], x_got.at[n], x_send.at[n], x_recv.at[n], x_peer)

    def add_x(k):
        x_copies[k].wait_recv()
        parts[mine(k)] = parts[mine(k)] + x_got[ORDER.index(k)]

    def send_z(n, src, dst, k):
        return remote(src, dst, z_send.at[n], z_recv.at[n], z_peer(k))

    def column_copy(j, source, owner):
        return pltpu.make_async_remote_copy(
            src_ref=q_mine.at[j], dst_ref=q_all.at[source, x_lo, core],
            send_sem=column_send.at[j], recv_sem=column_recv.at[source],
            device_id={"tensor": owner}, device_id_type=MESH,
        )

    def send_column(j):
        owner = dp * 4 + j

        @pl.when(owner == me)
        def _():
            q_all[me, x_lo, core] = q_mine[j]

        @pl.when(owner != me)
        def _():
            column_copy(j, me, owner).start()

    owns = me // 4 == dp
    my_rows = q_all.at[:, x_lo, core]

    def rows_copy(n, peer):
        return pltpu.make_async_remote_copy(
            src_ref=my_rows, dst_ref=my_rows, send_sem=q_send.at[n], recv_sem=q_recv.at[0],
            device_id=peer, device_id_type=MESH,
        )

    load_w_in.wait()
    load_w_out.wait()
    project(4)
    pl.semaphore_wait(barrier, len(peers) + core)
    send_x(4)

    @pl.when(core == 0)
    def _():
        pl.semaphore_signal(barrier, inc=1, device_id=core_peer, device_id_type=MESH)

    pl.semaphore_signal(here.at[0], inc=1, device_id=x_peer, device_id_type=MESH)
    load_query.wait()
    for j in range(4):
        q_mine[j] = query_v[:, j, :]
    project(1)
    near_up = send_z(0, parts.at[other(1)], near_got.at[0, 1 - a], 1)
    project(3)
    send_x(3)
    pl.semaphore_wait(here.at[0], 1)
    pl.semaphore_signal(here.at[1], inc=1, device_id=z_peer(2), device_id_type=MESH)
    pl.semaphore_signal(here.at[2], inc=1, device_id=z_peer(-2), device_id_type=MESH)
    project(-1)
    near_down = send_z(1, parts.at[other(-1)], near_got.at[1, 1 - a], -1)
    project(-3)
    send_x(-3)
    pl.semaphore_wait(here.at[1], 1)
    pl.semaphore_wait(here.at[2], 1)
    for j in range(4):
        send_column(j)
    add_x(4)
    four_up = send_z(2, parts.at[mine(4), 0:64], four_got.at[0], 2)
    four_down = send_z(3, parts.at[mine(4), 64:128], four_got.at[1], -2)
    project(2)
    send_x(2)
    project(-2)
    send_x(-2)
    project(0)
    near_up.wait_recv()
    near_down.wait_recv()
    parts[other(0)] = parts[other(0)] + near_got[0, 1 - a] + near_got[1, 1 - a]
    send_x(0)
    add_x(3)
    three_up = send_z(4, parts.at[mine(3)], three_got.at[0], 1)
    add_x(-3)
    three_down = send_z(5, parts.at[mine(-3)], three_got.at[1], -1)
    own_up = send_z(8, parts.at[mine(1)], near_got.at[0, a], 1)
    own_down = send_z(9, parts.at[mine(-1)], near_got.at[1, a], -1)

    @pl.when(owns)
    def _():
        for k in range(1, 16):
            source = lax.rem(me + k, 16)
            column_copy(0, source, source).wait_recv()
        for k in (1, 2, 3):
            rows_copy(k, dp_peer(k)).start()

    add_x(2)
    three_up.wait_recv()
    four_up.wait_recv()
    n = mine(2)
    parts[n, 0:64] = parts[n, 0:64] + three_got[0, 0:64] + four_got[0]
    parts[n, 64:128] = parts[n, 64:128] + three_got[0, 64:128]
    two_up = send_z(6, parts.at[n], two_got.at[0], 2)
    add_x(-2)
    three_down.wait_recv()
    four_down.wait_recv()
    n = mine(-2)
    parts[n, 0:64] = parts[n, 0:64] + three_got[1, 0:64]
    parts[n, 64:128] = parts[n, 64:128] + three_got[1, 64:128] + four_got[1]
    two_down = send_z(7, parts.at[n], two_got.at[1], -2)
    own_up.wait_recv()
    own_down.wait_recv()
    total = parts[mine(0)] + near_got[0, a] + near_got[1, a]
    load_mask.wait()
    load_f_out.wait()
    load_f_in.wait()
    f_blocks = f_out_v[...].reshape(16, 4, 64)
    for i in range(4):
        f_rows[16 * i : 16 * i + 16, :] = f_blocks[:, i, :]
    weights = jnp.zeros((1, 128), F32)
    for n in range(16):
        piece = mask_v[n // 4 : n // 4 + 1, 128 * (n % 4) : 128 * (n % 4) + 128].astype(F32)
        weights = jnp.where(me == n, piece / 512.0, weights)

    x_copies[0].wait_recv()
    total = total + x_got[ORDER.index(0)]
    two_up.wait_recv()
    total = total + two_got[0]
    two_down.wait_recv()
    total = total + two_got[1]

    side_out = jnp.dot(f_rows[...], total[64:128] * weights, precision=HIGH, preferred_element_type=F32)
    side_in = tn(f_in_v[...], total[0:64], HIGH)
    conditioned = nt(side_out, side_in, HIGH)

    for i in range(4):
        c_send[:, 64 * i : 64 * i + 64] = conditioned[16 * i : 16 * i + 16]
    far_first = [(k, row) for k in (4, 3, -3, 2, -2, 1, -1, 0) for row in (0, 1) if (k, row) != (0, 0)]
    c_copies = []
    for n, (k, row) in enumerate(far_first):
        peer = lax.rem(z + k + 8, 8) * 2 + (1 - a if row else a)
        c_copies.append(remote(c_send, c_got.at[me], c_send_sem.at[n], c_recv_sem.at[n], {"tensor": peer}))
    c_got[me] = c_send[...]


    @pl.when(jnp.logical_not(owns))
    def _():
        rows_copy(1, dp_peer(1)).wait_recv()

    lo_copy = remote(my_rows, my_rows, q_send.at[4], q_recv.at[1], lo_peer)
    lo_copy.wait_recv()
    block = q_all.at[:, :, core]
    core_copy = pltpu.make_async_remote_copy(
        src_ref=block, dst_ref=block, send_sem=q_send.at[5], recv_sem=q_recv.at[2],
        device_id=core_peer, device_id_type=MESH,
    )
    started.append(core_copy)

    @pl.when(core == 1)
    def _():
        core_copy.start()

    core_copy.wait_recv()

    @pl.when(core == 0)
    def _():
        core_copy.start()

    q = q_all[...].reshape(512, 256)
    high = q.astype(jnp.bfloat16)
    q_high[...] = high
    q_low[...] = (q - high.astype(F32)).astype(jnp.bfloat16)

    for j in range(4):

        @pl.when(dp * 4 + j != me)
        def _():
            column_copy(j, me, dp * 4 + j).wait_send()

    @pl.when(owns)
    def _():
        for k in (1, 2, 3):
            rows_copy(k, dp_peer(k)).wait_send()

    for copy in started:
        copy.wait_send()

    for copy in c_copies[::-1]:
        copy.wait_recv()
    got = c_got[...].reshape(4, 4, 16, 256)
    got = (got[:, 0] + got[:, 1] + got[:, 2] + got[:, 3]).reshape(64, 256)
    high = got.astype(jnp.bfloat16)
    low = (got - high.astype(F32)).astype(jnp.bfloat16)
    pairs = nt(high, q_high[...]) + (nt(high, q_low[...]) + nt(low, q_high[...]))
    left = lax.rem(lax.broadcasted_iota(jnp.int32, (64, 512), 0), 16)
    right = lax.broadcasted_iota(jnp.int32, (64, 512), 1) // 32
    pairs = jnp.where(left == right, pairs, 0.0).reshape(4, 16, 512)
    scores = jnp.sum(pairs, axis=1)
    scores = scores[:, 0:128] + scores[:, 128:256] + scores[:, 256:384] + scores[:, 384:512]
    out[...] = scores[:, 0:32] + scores[:, 32:64] + scores[:, 64:96] + scores[:, 96:128]


def local(act, grads, mask, w_in, w_out, f_out, f_in, query):
    docs, length, hidden = act.shape
    model = grads.shape[2]
    vmem, sem = pltpu.VMEM, pltpu.SemaphoreType.DMA
    scores = pl.pallas_call(
        kernel,
        name="influence",
        out_shape=jax.ShapeDtypeStruct((4, 32), F32),
        in_specs=[pl.BlockSpec(memory_space=pl.ANY)] * 8,
        out_specs=pl.BlockSpec(memory_space=pltpu.VMEM),
        scratch_shapes=[
            vmem((8, 256, hidden), jnp.bfloat16),
            vmem((8, 256, model), jnp.bfloat16),
            vmem((4, 512), jnp.int32),
            vmem((64, hidden), jnp.bfloat16),
            vmem((64, model), jnp.bfloat16),
            vmem((64, 64), F32),
            vmem((64, 64), F32),
            vmem((8, 4, 256), F32),
            vmem((64, 64), F32),
            vmem((16, 128, 128), F32),
            vmem((8, 128, 128), F32),
            vmem((2, 2, 128, 128), F32),
            vmem((2, 128, 128), F32),
            vmem((2, 64, 128), F32),
            vmem((2, 128, 128), F32),
            vmem((4, 8, 256), F32),
            vmem((16, 2, 2, 8, 256), F32),
            vmem((512, 256), jnp.bfloat16),
            vmem((512, 256), jnp.bfloat16),
            vmem((16, 256), F32),
            vmem((16, 16, 256), F32),
            sem((23,)),
            sem((8,)), sem((8,)),
            sem((10,)), sem((10,)),
            sem((6,)), sem((3,)),
            sem((4,)), sem((16,)),
            sem((15,)), sem((15,)),
            pltpu.SemaphoreType.REGULAR((3,)),
        ],
        compiler_params=pltpu.CompilerParams(
            collective_id=0, has_side_effects=True, vmem_limit_bytes=56549376
        ),
    )(
        act.reshape(docs * length, hidden),
        grads.reshape(docs * length, model),
        mask, w_in.T, w_out.T, f_out, f_in, query,
    )
    return scores.reshape(4, 32, 1)


def solution(mesh):
    placed = (
        P(("dp", "query"), None, "tensor"),
        P(("dp", "query"), None, "tensor"),
        P(("dp", "query"), None),
        P("tensor", None),
        P("tensor", None),
        P(),
        P(),
        P("query", "dp", "tensor"),
    )
    return jax.shard_map(
        local,
        mesh=mesh,
        in_specs=placed,
        out_specs=P(("dp", "query"), None, "tensor"),
        check_vma=False,
    )
```

```python
import functools

import jax
import jax.numpy as jnp
from jax import lax
from jax.experimental import pallas as pl
from jax.experimental.pallas import tpu as pltpu
from jax.sharding import PartitionSpec as P

MESH = pl.DeviceIdType.MESH
F32 = jnp.float32
ORDER = (4, 1, 3, -1, -3, 2, -2, 0)


def nt(a, b, precision=None):
    return lax.dot_general(
        a, b, (((1,), (1,)), ((), ())), precision=precision, preferred_element_type=F32
    )


def tn(a, b, precision=None):
    return lax.dot_general(
        a, b, (((0,), (0,)), ((), ())), precision=precision, preferred_element_type=F32
    )


def three(product, p, q):
    p_high, q_high = p.astype(jnp.bfloat16), q.astype(jnp.bfloat16)
    p_low = (p - p_high.astype(F32)).astype(jnp.bfloat16)
    q_low = (q - q_high.astype(F32)).astype(jnp.bfloat16)
    return product(p_high, q_high) + (product(p_high, q_low) + product(p_low, q_high))


def kernel(
    act, grads, mask, w_in, w_out, f_out, f_in, query, out,
    act_v, grads_v, mask_v, w_in_v, w_out_v, f_out_v, f_in_v, query_v,
    f_rows, parts, x_got, near_got, three_got, four_got, two_got,
    q_mine, q_all, q_high, q_low, c_send, c_got,
    load_sem, x_send, x_recv, z_send, z_recv, q_send, q_recv, column_send, column_recv,
    c_send_sem, c_recv_sem, here,
):
    dp = lax.axis_index("dp")
    me = lax.axis_index("tensor")
    qi = lax.axis_index("query")
    z, a = me // 2, lax.rem(me, 2)
    x_lo, core = qi // 2, lax.rem(qi, 2)

    def dp_peer(k):
        return {"dp": lax.rem(dp + k, 4)}

    def z_peer(k):
        return {"tensor": lax.rem(z + k + 8, 8) * 2 + a}

    lo_peer = {"query": (1 - x_lo) * 2 + core}
    core_peer = {"query": x_lo * 2 + 1 - core}
    x_peer = {"tensor": z * 2 + 1 - a}

    barrier = pltpu.get_barrier_semaphore()
    peers = [x_peer] + [z_peer(k) for k in (2, -2)] + [dp_peer(k) for k in (2, 1, 3)]
    peers += [z_peer(k) for k in (1, -1)] + [lo_peer]
    for peer in peers:
        pl.semaphore_signal(barrier, inc=1, device_id=peer, device_id_type=MESH)


    def load(src, dst, n):
        copy = pltpu.make_async_copy(src, dst, load_sem.at[n])
        copy.start(priority=1)
        return copy

    load_w_in = load(w_in, w_in_v, 0)
    load_w_out = load(w_out, w_out_v, 1)
    load_rows = []
    for n, k in enumerate(ORDER):
        owner = lax.rem(z + k + 8, 8)
        rows = pl.ds(pl.multiple_of(owner * 256, 256), 256)
        load_rows.append(
            (
                load(act.at[rows], act_v.at[n], 7 + 2 * n),
                load(grads.at[rows], grads_v.at[n], 8 + 2 * n),
            )
        )
        if n == 0:
            load_query = load(query, query_v, 2)
    load_mask = load(mask, mask_v, 3)
    load_f_out = load(f_out, f_out_v, 4)
    load_f_in = load(f_in, f_in_v, 5)

    started = []

    def remote(src, dst, send, recv, peer):
        copy = pltpu.make_async_remote_copy(
            src_ref=src, dst_ref=dst, send_sem=send, recv_sem=recv, device_id=peer, device_id_type=MESH
        )
        copy.start()
        started.append(copy)
        return copy

    def project(k):
        n = ORDER.index(k)
        for copy in load_rows[n]:
            copy.wait()
        p_in = nt(w_in_v[...], act_v[n])
        p_out = nt(w_out_v[...], grads_v[n])
        for half in range(2):
            lanes = slice(128 * half, 128 * half + 128)
            parts[2 * n + half, 0:64, :] = p_in[:, lanes]
            parts[2 * n + half, 64:128, :] = p_out[:, lanes]

    def mine(k):
        return 2 * ORDER.index(k) + a

    def other(k):
        return 2 * ORDER.index(k) + 1 - a

    x_copies = {}

    def send_x(k):
        n = ORDER.index(k)
        x_copies[k] = remote(parts.at[other(k)], x_got.at[n], x_send.at[n], x_recv.at[n], x_peer)

    def add_x(k):
        x_copies[k].wait_recv()
        parts[mine(k)] = parts[mine(k)] + x_got[ORDER.index(k)]

    def send_z(n, src, dst, k):
        return remote(src, dst, z_send.at[n], z_recv.at[n], z_peer(k))

    def column_copy(j, source, owner):
        return pltpu.make_async_remote_copy(
            src_ref=q_mine.at[j], dst_ref=q_all.at[source, x_lo, core],
            send_sem=column_send.at[j], recv_sem=column_recv.at[source],
            device_id={"tensor": owner}, device_id_type=MESH,
        )

    def send_column(j):
        owner = dp * 4 + j

        @pl.when(owner == me)
        def _():
            q_all[me, x_lo, core] = q_mine[j]

        @pl.when(owner != me)
        def _():
            column_copy(j, me, owner).start()

    owns = me // 4 == dp
    my_rows = q_all.at[:, x_lo, core]

    def rows_copy(n, peer):
        return pltpu.make_async_remote_copy(
            src_ref=my_rows, dst_ref=my_rows, send_sem=q_send.at[n], recv_sem=q_recv.at[0],
            device_id=peer, device_id_type=MESH,
        )

    load_w_in.wait()
    load_w_out.wait()
    project(4)
    pl.semaphore_wait(barrier, len(peers) + core)
    send_x(4)

    @pl.when(core == 0)
    def _():
        pl.semaphore_signal(barrier, inc=1, device_id=core_peer, device_id_type=MESH)

    pl.semaphore_signal(here.at[0], inc=1, device_id=x_peer, device_id_type=MESH)
    load_query.wait()
    for j in range(4):
        q_mine[j] = query_v[:, j, :]
    project(1)
    near_up = send_z(0, parts.at[other(1)], near_got.at[0, 1 - a], 1)
    project(3)
    send_x(3)
    pl.semaphore_wait(here.at[0], 1)
    pl.semaphore_signal(here.at[1], inc=1, device_id=z_peer(2), device_id_type=MESH)
    pl.semaphore_signal(here.at[2], inc=1, device_id=z_peer(-2), device_id_type=MESH)
    project(-1)
    near_down = send_z(1, parts.at[other(-1)], near_got.at[1, 1 - a], -1)
    project(-3)
    send_x(-3)
    pl.semaphore_wait(here.at[1], 1)
    pl.semaphore_wait(here.at[2], 1)
    for j in range(4):
        send_column(j)
    add_x(4)
    four_up = send_z(2, parts.at[mine(4), 0:64], four_got.at[0], 2)
    four_down = send_z(3, parts.at[mine(4), 64:128], four_got.at[1], -2)
    project(2)
    send_x(2)
    project(-2)
    send_x(-2)
    project(0)
    near_up.wait_recv()
    near_down.wait_recv()
    parts[other(0)] = parts[other(0)] + near_got[0, 1 - a] + near_got[1, 1 - a]
    send_x(0)
    add_x(3)
    three_up = send_z(4, parts.at[mine(3)], three_got.at[0], 1)
    add_x(-3)
    three_down = send_z(5, parts.at[mine(-3)], three_got.at[1], -1)
    own_up = send_z(8, parts.at[mine(1)], near_got.at[0, a], 1)
    own_down = send_z(9, parts.at[mine(-1)], near_got.at[1, a], -1)

    @pl.when(owns)
    def _():
        for k in range(1, 16):
            source = lax.rem(me + k, 16)
            column_copy(0, source, source).wait_recv()
        for k in (1, 2, 3):
            rows_copy(k, dp_peer(k)).start()

    add_x(2)
    three_up.wait_recv()
    four_up.wait_recv()
    n = mine(2)
    parts[n, 0:64] = parts[n, 0:64] + three_got[0, 0:64] + four_got[0]
    parts[n, 64:128] = parts[n, 64:128] + three_got[0, 64:128]
    two_up = send_z(6, parts.at[n], two_got.at[0], 2)
    add_x(-2)
    three_down.wait_recv()
    four_down.wait_recv()
    n = mine(-2)
    parts[n, 0:64] = parts[n, 0:64] + three_got[1, 0:64]
    parts[n, 64:128] = parts[n, 64:128] + three_got[1, 64:128] + four_got[1]
    two_down = send_z(7, parts.at[n], two_got.at[1], -2)
    own_up.wait_recv()
    own_down.wait_recv()
    total = parts[mine(0)] + near_got[0, a] + near_got[1, a]
    load_mask.wait()
    load_f_out.wait()
    load_f_in.wait()
    f_blocks = f_out_v[...].reshape(16, 4, 64)
    for i in range(4):
        f_rows[16 * i : 16 * i + 16, :] = f_blocks[:, i, :]
    weights = jnp.zeros((1, 128), F32)
    for n in range(16):
        piece = mask_v[n // 4 : n // 4 + 1, 128 * (n % 4) : 128 * (n % 4) + 128].astype(F32)
        weights = jnp.where(me == n, piece / 512.0, weights)

    x_copies[0].wait_recv()
    total = total + x_got[ORDER.index(0)]
    two_up.wait_recv()
    total = total + two_got[0]
    two_down.wait_recv()
    total = total + two_got[1]

    side_out = three(lambda p, q: jnp.dot(p, q, preferred_element_type=F32), f_rows[...], total[64:128] * weights)
    side_in = three(tn, f_in_v[...], total[0:64])
    conditioned = three(nt, side_out, side_in)

    for i in range(4):
        c_send[:, 64 * i : 64 * i + 64] = conditioned[16 * i : 16 * i + 16]
    far_first = [(k, row) for k in (4, 3, -3, 2, -2, 1, -1, 0) for row in (0, 1) if (k, row) != (0, 0)]
    c_copies = []
    for n, (k, row) in enumerate(far_first):
        peer = lax.rem(z + k + 8, 8) * 2 + (1 - a if row else a)
        c_copies.append(remote(c_send, c_got.at[me], c_send_sem.at[n], c_recv_sem.at[n], {"tensor": peer}))
    c_got[me] = c_send[...]


    @pl.when(jnp.logical_not(owns))
    def _():
        rows_copy(1, dp_peer(1)).wait_recv()

    lo_copy = remote(my_rows, my_rows, q_send.at[4], q_recv.at[1], lo_peer)
    lo_copy.wait_recv()
    block = q_all.at[:, :, core]
    core_copy = pltpu.make_async_remote_copy(
        src_ref=block, dst_ref=block, send_sem=q_send.at[5], recv_sem=q_recv.at[2],
        device_id=core_peer, device_id_type=MESH,
    )
    started.append(core_copy)

    @pl.when(core == 1)
    def _():
        core_copy.start()

    core_copy.wait_recv()

    @pl.when(core == 0)
    def _():
        core_copy.start()

    q = q_all[...].reshape(512, 256)
    high = q.astype(jnp.bfloat16)
    q_high[...] = high
    q_low[...] = (q - high.astype(F32)).astype(jnp.bfloat16)

    for j in range(4):

        @pl.when(dp * 4 + j != me)
        def _():
            column_copy(j, me, dp * 4 + j).wait_send()

    @pl.when(owns)
    def _():
        for k in (1, 2, 3):
            rows_copy(k, dp_peer(k)).wait_send()

    for copy in started:
        copy.wait_send()

    for copy in c_copies[::-1]:
        copy.wait_recv()
    got = c_got[...].reshape(4, 4, 16, 256)
    got = (got[:, 0] + got[:, 1] + got[:, 2] + got[:, 3]).reshape(64, 256)
    high = got.astype(jnp.bfloat16)
    low = (got - high.astype(F32)).astype(jnp.bfloat16)
    pairs = nt(high, q_high[...]) + (nt(high, q_low[...]) + nt(low, q_high[...]))
    left = lax.rem(lax.broadcasted_iota(jnp.int32, (64, 512), 0), 16)
    right = lax.broadcasted_iota(jnp.int32, (64, 512), 1) // 32
    pairs = jnp.where(left == right, pairs, 0.0).reshape(4, 16, 512)
    scores = jnp.sum(pairs, axis=1)
    scores = scores[:, 0:128] + scores[:, 128:256] + scores[:, 256:384] + scores[:, 384:512]
    out[...] = scores[:, 0:32] + scores[:, 32:64] + scores[:, 64:96] + scores[:, 96:128]


def local(act, grads, mask, w_in, w_out, f_out, f_in, query):
    docs, length, hidden = act.shape
    model = grads.shape[2]
    vmem, sem = pltpu.VMEM, pltpu.SemaphoreType.DMA
    scores = pl.pallas_call(
        kernel,
        name="influence",
        out_shape=jax.ShapeDtypeStruct((4, 32), F32),
        in_specs=[pl.BlockSpec(memory_space=pl.ANY)] * 8,
        out_specs=pl.BlockSpec(memory_space=pltpu.VMEM),
        scratch_shapes=[
            vmem((8, 256, hidden), jnp.bfloat16),
            vmem((8, 256, model), jnp.bfloat16),
            vmem((4, 512), jnp.int32),
            vmem((64, hidden), jnp.bfloat16),
            vmem((64, model), jnp.bfloat16),
            vmem((64, 64), F32),
            vmem((64, 64), F32),
            vmem((8, 4, 256), F32),
            vmem((64, 64), F32),
            vmem((16, 128, 128), F32),
            vmem((8, 128, 128), F32),
            vmem((2, 2, 128, 128), F32),
            vmem((2, 128, 128), F32),
            vmem((2, 64, 128), F32),
            vmem((2, 128, 128), F32),
            vmem((4, 8, 256), F32),
            vmem((16, 2, 2, 8, 256), F32),
            vmem((512, 256), jnp.bfloat16),
            vmem((512, 256), jnp.bfloat16),
            vmem((16, 256), F32),
            vmem((16, 16, 256), F32),
            sem((23,)),
            sem((8,)), sem((8,)),
            sem((10,)), sem((10,)),
            sem((6,)), sem((3,)),
            sem((4,)), sem((16,)),
            sem((15,)), sem((15,)),
            pltpu.SemaphoreType.REGULAR((3,)),
        ],
        compiler_params=pltpu.CompilerParams(
            collective_id=0, has_side_effects=True, vmem_limit_bytes=56549376
        ),
    )(
        act.reshape(docs * length, hidden),
        grads.reshape(docs * length, model),
        mask, w_in.T, w_out.T, f_out, f_in, query,
    )
    return scores.reshape(4, 32, 1)


def solution(mesh):
    placed = (
        P(("dp", "query"), None, "tensor"),
        P(("dp", "query"), None, "tensor"),
        P(("dp", "query"), None),
        P("tensor", None),
        P("tensor", None),
        P(),
        P(),
        P("query", "dp", "tensor"),
    )
    return jax.shard_map(
        local,
        mesh=mesh,
        in_specs=placed,
        out_specs=P(("dp", "query"), None, "tensor"),
        check_vma=False,
    )
```
